128 devices in a mesh: grp: 2 (over x_lo), dev: 32 (over x_hi, z, y), sub: 2 (over core).
Axes of the slice: x: 4 (x_hi: 2, x_lo: 2; x = x_hi * 2 + x_lo), y: 4, z: 4, core: 2. Of those that a mesh axis runs over, the one named last changes fastest.
Arguments:
- queries: bfloat16 [320, 8192], P(('grp', 'dev'), 'sub'), may hold values from -200 to 200
- new_keys: bfloat16 [320, 512], P(('grp', 'dev'), 'sub'), may hold values from -6 to 6
- new_values: bfloat16 [320, 512], P(('grp', 'dev'), 'sub'), may hold values from -6 to 6
- key_cache: bfloat16 [320, 384, 512], P(('grp', 'dev'), None, 'sub'), may hold values from -6 to 6
- value_cache: bfloat16 [320, 384, 512], P(('grp', 'dev'), None, 'sub'), may hold values from -6 to 6
- lengths: int32 [320], P(('grp', 'dev')), may hold values from 1 to 384, as said below
- residual: bfloat16 [320, 16384], P('grp', ('dev', 'sub')), may hold values from -6 to 6
- o_weight: bfloat16 [8192, 16384], P('sub', 'dev'), may hold values from -0.5 to 0.5
- norm_gain: bfloat16 [16384], P(('dev', 'sub')), may hold values from 0.5 to 1.5
- w_gate: bfloat16 [26624, 16384], P(('grp', 'dev', 'sub')), may hold values from -0.046875 to 0.046875
- w_up: bfloat16 [26624, 16384], P(('grp', 'dev', 'sub')), may hold values from -0.046875 to 0.046875
- w_down: bfloat16 [26624, 16384], P(('grp', 'dev', 'sub')), may hold values from -0.125 to 0.125
Outputs:
- layer_out: bfloat16 [320, 16384], P('grp', ('dev', 'sub'))
The draws below stay inside these ranges and needn't reach their ends.
Inputs may be any that keep to these rules, and one draw needn't show every extreme that they name: `lengths`: some request uses all 384 positions.
All inputs are finite; a program needn't handle non-finite values.
Results may differ from the reference program's by a relative error of at most 0.015.
Values may be sent and summed in bfloat16 or wider, within the bound.
A program may use at most 128 MiB of HBM per device.

```python
import jax
import jax.numpy as jnp
from jax import lax

D = 16384
FF = 26624
HEADS = 64
KV_HEADS = 4
HEAD_DIM = 128
CACHE = 384
REQUESTS = 320


def draw_queries(key, part):
    key = jax.random.fold_in(key, 11)
    values = jax.random.normal(key, (REQUESTS, HEADS * HEAD_DIM), jnp.float32)
    values = jnp.clip(values, -6.0, 6.0)
    return values.astype(jnp.bfloat16)


def draw_lengths(key, part):
    key = jax.random.fold_in(key, 23)
    drawn = jax.random.randint(key, (REQUESTS,), 1, CACHE + 1, jnp.int32)
    chosen = jax.random.randint(jax.random.fold_in(key, 5), (), 0, REQUESTS, jnp.int32)
    positions = jnp.arange(REQUESTS, dtype=jnp.int32)
    return jnp.where(positions == chosen, jnp.int32(CACHE), drawn).astype(jnp.int32)


def strengthened(values, stream_key, source, target, blocks, factor):
    owner, partner = [(jnp.arange(values.shape[axis_at]) // (values.shape[axis_at] // blocks)).reshape([-1 if axis == axis_at else 1 for axis in range(values.ndim)]) for axis_at in (source, target)]
    chosen = jax.random.permutation(stream_key, blocks)[partner]
    strong = (owner == chosen) | (owner == (partner + blocks // 2) % blocks)
    return jnp.where(strong, factor * values, values)


def block_levels(rng, dims, split, smallest, largest):
    level = 1.0
    for axis_at, shards_of in split:
        steps = jax.random.uniform(jax.random.fold_in(jax.random.fold_in(rng, 6), axis_at), (shards_of,), jnp.float32, smallest / len(split), largest / len(split))
        level = level * jnp.repeat(jnp.exp(steps), dims[axis_at] // shards_of).reshape((-1,) + (1,) * (len(dims) - 1 - axis_at))
    return level


def scatter_about(key, shape, scale, most, cuts=(), held_as=jnp.bfloat16):
    factor_of = block_levels(key, shape, cuts, -0.22, 0.18) if cuts else 1.0
    result = jax.random.normal(key, shape, jnp.float32) * scale * factor_of
    return jnp.minimum(jnp.maximum(result, -most), most).astype(held_as)


def noise_with(key, shape, width, limit, split, heavy, held_as=jnp.bfloat16):
    values = width * jax.random.normal(key, shape, jnp.float32)
    if split:
        values = values * block_levels(key, shape, split, -0.22, 0.18)
    return jnp.clip(strengthened(values, jax.random.fold_in(key, 3), *heavy), -limit, limit).astype(held_as)


def setup_inputs(seed: int = 0) -> dict:
    splits = jax.random.split(jax.random.key(seed), 13)
    return {
        "queries": draw_queries(jax.random.fold_in(splits[12], 71), 0),
        "new_keys": scatter_about(splits[1], (REQUESTS, KV_HEADS * HEAD_DIM), 1.0, 6.0, ((0, 64), (1, 2))),
        "new_values": scatter_about(splits[2], (REQUESTS, KV_HEADS * HEAD_DIM), 1.0, 6.0, ((0, 64), (1, 2))),
        "key_cache": scatter_about(splits[3], (REQUESTS, CACHE, KV_HEADS * HEAD_DIM), 1.0, 6.0, ((0, 64), (2, 2))),
        "value_cache": scatter_about(splits[4], (REQUESTS, CACHE, KV_HEADS * HEAD_DIM), 1.0, 6.0, ((0, 64), (2, 2))),
        "lengths": draw_lengths(jax.random.fold_in(splits[12], 71), 0),
        "residual": scatter_about(splits[6], (REQUESTS, D), 1.0, 6.0, ((0, 2), (1, 64))),
        "o_weight": scatter_about(splits[7], (HEADS * HEAD_DIM, D), HEAD_DIM ** -0.5, 0.5, ((0, 2), (1, 32))),
        "norm_gain": jnp.clip(0.5 + 1.0 * jax.random.uniform(splits[8], (D,), jnp.float32) ** block_levels(splits[8], (D,), ((0, 64),), -0.2, 0.2), 0.5, 1.5).astype(jnp.bfloat16),
        "w_gate": scatter_about(splits[9], (FF, D), D ** -0.5, 0.046875, ((0, 128),)),
        "w_up": scatter_about(splits[10], (FF, D), D ** -0.5, 0.046875, ((0, 128),)),
        "w_down": noise_with(splits[11], (FF, D), FF ** -0.5, 0.125, ((0, 128),), (0, 1, 128, 5.5)),
    }


def reference(queries, new_keys, new_values, key_cache, value_cache, lengths, residual, o_weight, norm_gain, w_gate, w_up, w_down):
    per_group = HEADS // KV_HEADS
    rescale_factor = 1.0 / HEAD_DIM ** 0.5
    query_float = queries.astype(jnp.float32).reshape(REQUESTS, KV_HEADS, per_group, HEAD_DIM)
    keys_f = key_cache.astype(jnp.float32).reshape(REQUESTS, CACHE, KV_HEADS, HEAD_DIM)
    values_f = value_cache.astype(jnp.float32).reshape(REQUESTS, CACHE, KV_HEADS, HEAD_DIM)
    new_key_float = new_keys.astype(jnp.float32).reshape(REQUESTS, KV_HEADS, HEAD_DIM)
    newv_f = new_values.astype(jnp.float32).reshape(REQUESTS, KV_HEADS, HEAD_DIM)
    attention_scores = jnp.einsum('bkgd,blkd->bkgl', query_float, keys_f) * rescale_factor
    self_key_score = jnp.einsum('uyvz,uyz->uyv', query_float, new_key_float) * rescale_factor
    valid = (jnp.arange(CACHE, dtype=jnp.int32)[None, :] < lengths[:, None])[:, None, None, :]
    masked = jnp.where(valid, attention_scores, jnp.float32(-1e+30))
    top_score = jnp.maximum(lax.optimization_barrier(jnp.max(masked, axis=3)), self_key_score)
    weights = jnp.where(valid, jnp.exp(masked - top_score[..., None]), jnp.float32(0.0))
    own_weight = jnp.exp(self_key_score - top_score)
    total = lax.optimization_barrier(jnp.sum(weights, axis=3)) + own_weight
    probs = (weights / total[..., None]).astype(jnp.bfloat16)
    own_probs = (own_weight / total).astype(jnp.bfloat16)
    context = jnp.einsum('bkgl,blkd->bkgd', probs.astype(jnp.float32), values_f)
    context = context + own_probs.astype(jnp.float32)[..., None] * newv_f[:, :, None, :]
    context = context.astype(jnp.bfloat16).reshape(REQUESTS, HEADS * HEAD_DIM)
    middle_hidden = residual.astype(jnp.float32) + jnp.dot(context, o_weight, preferred_element_type=jnp.float32)
    inverse = lax.rsqrt(lax.optimization_barrier(jnp.mean(middle_hidden * middle_hidden, axis=1, keepdims=True)) + 1e-05)
    normed = (middle_hidden * inverse * norm_gain.astype(jnp.float32)[None, :]).astype(jnp.bfloat16)
    contract = (((1,), (1,)), ((), ()))
    gate_sum = lax.dot_general(normed, w_gate, contract, preferred_element_type=jnp.float32)
    up_sum = lax.dot_general(normed, w_up, contract, preferred_element_type=jnp.float32)
    hidden = (jax.nn.silu(gate_sum) * up_sum).astype(jnp.bfloat16)
    output = middle_hidden + jnp.dot(hidden, w_down, preferred_element_type=jnp.float32)
    return output.astype(jnp.bfloat16)
```

```python
import functools

import jax
import jax.numpy as jnp
from jax import lax
from jax.experimental import pallas as pl
from jax.experimental.pallas import tpu as pltpu
from jax.sharding import PartitionSpec as P

D = 16384
HEAD_DIM = 128
MESH = pl.DeviceIdType.MESH
F32, BF16 = jnp.float32, jnp.bfloat16
ROWS, HID = 160, 208
CHUNKS = {"0": (0, 0), "1": (slice(1, 4), 0), "2": (0, slice(1, 4)), "3": (slice(1, 4), slice(1, 4))}
PARTS = (
    ((0, 1, 2), 0, (0, 112), ((0, (0, 64)), (0, (64, 112)))),
    ((1, 2, 0), 1, (0, 112), ((1, (0, 64)), (1, (64, 112)))),
    ((2, 0, 1), slice(0, 2), (112, 160), ((0, (112, 160)), (1, (112, 160)))),
)


def place():
    grp, dev, sub = lax.axis_index("grp"), lax.axis_index("dev"), lax.axis_index("sub")
    return [(dev // 16) * 2 + grp, dev % 4, (dev // 4) % 4], sub


def device(at, sub):
    x, y, z = at
    return (lax.rem(x, 2), (x // 2) * 16 + z * 4 + y, sub)


def shifted(at, dim, by):
    at = list(at)
    at[dim] = lax.rem(at[dim] + by, 4)
    return at


class Wires:
    def __init__(self, at, sub, send, recv):
        self.at, self.sub, self.send, self.recv, self.n = at, sub, send, recv, 0
        self.started = []

    def post(self, src, dst, dim, by):
        if dim is None:
            to = device(self.at, 1 - self.sub)
        else:
            to = device(shifted(self.at, dim, by), self.sub)
        copy = pltpu.make_async_remote_copy(
            src_ref=src, dst_ref=dst, send_sem=self.send.at[self.n], recv_sem=self.recv.at[self.n],
            device_id=to, device_id_type=MESH,
        )
        copy.start()
        self.n += 1
        self.started.append(copy)
        return copy

    def drain(self):
        for copy in self.started:
            copy.wait_send()
        self.started = []


def block(buf, part, a, b, c, tail=(), half=None):
    dims, h, rows, halves = PARTS[part]
    if half is not None:
        h, rows = halves[half]
    idx = [None] * 3
    idx[dims[0]], idx[dims[1]], idx[dims[2]] = a, b, c
    return buf.at[tuple(idx) + tuple(tail) + (h, slice(*rows), slice(None))]


def lay(part, a, b):
    return (b, a) if part == 2 else (a, b)


def flat(buf, part, lead, half=None):
    _, h, rows, halves = PARTS[part]
    if half is not None:
        h, rows = halves[half]
    return buf.at[tuple(lead) + (h, slice(*rows), slice(None))]


def gather(w, XB, sq, ready):
    m1, m2a, m2b, m3, fwd = {}, {}, {}, {}, {}
    own = lambda p: block(XB, p, 0, 0, 0, (0,))
    xb = lambda p, a, b, c, half=None, s=0: block(XB, p, a, b, c, (s,), half)
    d2d = []

    def plane(p, c, up=True):
        a, b = CHUNKS[c]
        d3 = PARTS[p][0][2]
        m3[p, c] = [
            w.post(xb(p, a, b, 0), xb(p, a, b, 3), d3, 1),
            w.post(xb(p, a, b, 0), xb(p, a, b, 1), d3, 3),
        ]

    def onward(p, c):
        a, b = CHUNKS[c]
        d3 = PARTS[p][0][2]
        for copy in m3[p, c]:
            copy.wait_recv()
        fwd[p, c] = [
            w.post(xb(p, a, b, 3, 0), xb(p, a, b, 2, 0), d3, 1),
            w.post(xb(p, a, b, 1, 1), xb(p, a, b, 2, 1), d3, 3),
        ]

    def across(p, a, b, c):
        d2d.append(w.post(xb(p, a, b, c), xb(p, a, b, c, s=1), None, 0))

    for p in range(3):
        d1 = PARTS[p][0][0]
        m1[p] = [w.post(own(p), xb(p, 4 - k, 0, 0), d1, k) for k in (1, 3, 2)]
    for p in range(3):
        d2 = PARTS[p][0][1]
        m2a[p] = [w.post(own(p), xb(p, 0, 4 - k, 0), d2, k) for k in (1, 3, 2)]
    for p in range(3):
        plane(p, "0")
    sq(0)
    for p in range(3):
        d2 = PARTS[p][0][1]
        for copy in m1[p]:
            copy.wait_recv()
        m2b[p] = [w.post(xb(p, slice(1, 4), 0, 0), xb(p, slice(1, 4), 4 - k, 0), d2, k) for k in (1, 3, 2)]
        plane(p, "1")
        across(p, slice(0, 4), 0, 0)
    for p in range(3):
        for copy in m2a[p]:
            copy.wait_recv()
        plane(p, "2")
    sq(1)
    for p in range(3):
        onward(p, "0")
    for p in range(3):
        for copy in m2b[p]:
            copy.wait_recv()
        plane(p, "3")
        across(p, slice(0, 4), slice(1, 4), 0)
    sq(2)
    for p in range(3):
        onward(p, "1")
    for p in range(3):
        onward(p, "2")
    sq(3)
    ready(0)
    for p in range(3):
        onward(p, "3")
        across(p, slice(0, 4), slice(0, 4), 1)
        across(p, slice(0, 4), slice(0, 4), 3)
    sq(4)
    ready(1)
    for p in range(3):
        for c in "0123":
            for copy in fwd[p, c]:
                copy.wait_recv()
        across(p, slice(0, 4), slice(0, 4), 2)
    for copy in d2d:
        copy.wait_recv()
    ready(2)


def ffn_kernel(mid_ref, gain_ref, wg_hbm, wu_hbm, wd_hbm, out_ref,
               XB, PB, SB, RB, FB, G1, G3, HB, JB, sqs, sqr, wg, wu, wd, acc, hid, wsem, send, recv):
    at, sub = place()
    x0, y0, z0 = at
    grp = lax.rem(x0, 2)
    w = Wires(at, sub, send, recv)
    loads = [pltpu.make_async_copy(a, b, wsem.at[i]) for i, (a, b) in enumerate(((wg_hbm, wg), (wu_hbm, wu), (wd_hbm, wd)))]
    for load in loads:
        load.start()
    barrier = pltpu.get_barrier_semaphore()
    for dim in range(3):
        for by in (1, 2, 3):
            pl.semaphore_signal(barrier, inc=1, device_id=device(shifted(at, dim, by), sub), device_id_type=MESH)
    pl.semaphore_signal(barrier, inc=1, device_id=device(at, 1 - sub), device_id_type=MESH)

    mid = mid_ref[...]
    rows = (mid * gain_ref[...].astype(F32)).astype(BF16)
    XB[0, 0, 0, 0, 0] = rows[:, :128]
    XB[0, 0, 0, 0, 1] = rows[:, 128:]
    eye = lax.broadcasted_iota(jnp.int32, (ROWS, 256), 0) == lax.broadcasted_iota(jnp.int32, (ROWS, 256), 1)
    column = jnp.sum(mid * mid, axis=1, keepdims=True)
    sqs[0] = jnp.broadcast_to(jnp.sum(jnp.where(eye, column, 0.0), axis=0, keepdims=True), (8, 256))
    pl.semaphore_wait(barrier, 10)

    sq_copies = {}

    def sq(step):
        if step > 0:
            total = sqs[step - 1]
            for i, copy in enumerate(sq_copies[step - 1]):
                copy.wait_recv()
                total = total + sqr[(step - 1) * 3 + i]
            sqs[step] = total
        if step == 0:
            sq_copies[0] = [w.post(sqs.at[0], sqr.at[0], None, 0)]
        elif step == 1:
            sq_copies[1] = [w.post(sqs.at[1], sqr.at[3 + i], 1, k) for i, k in enumerate((1, 3, 2))]
        elif step == 2:
            sq_copies[2] = [w.post(sqs.at[2], sqr.at[6 + i], 2, k) for i, k in enumerate((1, 3, 2))]
        elif step == 3:
            sq_copies[3] = [w.post(sqs.at[3], sqr.at[9], 0, 2)]
        else:
            sq_copies[4] = [w.post(sqs.at[4], sqr.at[12], 0, 1)]

    def dev_at(rx, ry, rz):
        return (lax.rem(x0 + rx, 4) // 2) * 16 + lax.rem(z0 + rz, 4) * 4 + lax.rem(y0 + ry, 4)

    def ready(step):
        if step != 2:
            return
        loads[0].wait()
        loads[1].wait()
        acc[...] = jnp.zeros_like(acc)

        @pl.loop(0, 32)
        def _(i):
            rx, ry, rz = (i // 16) * 2, (i // 4) % 4, i % 4
            other = lax.rem(rx + 5 - 2 * grp, 4)
            k = pl.multiple_of(dev_at(rx, ry, rz) * 512, 512)
            lhs = jnp.concatenate(
                [
                    jnp.concatenate([XB[q, ry, rz, s, h] for s in (sub, 1 - sub) for h in (0, 1)], axis=1)
                    for q in (rx, other)
                ],
                axis=0,
            )
            for j, weight in enumerate((wg, wu)):
                acc[j] += lax.dot_general(
                    lhs, weight[:, pl.ds(k, 512)], (((1,), (1,)), ((), ())), preferred_element_type=F32
                )

    gather(w, XB, sq, ready)

    sq_copies[4][0].wait_recv()
    for i, sums in enumerate((sqs[4], sqr[12])):
        inv_row = lax.rsqrt(sums[0:1] / D + 1e-05)
        inv = jnp.sum(jnp.where(eye, inv_row, 0.0), axis=1, keepdims=True)
        gate = acc[0, i * ROWS:(i + 1) * ROWS] * inv
        up = acc[1, i * ROWS:(i + 1) * ROWS] * inv
        hid[i] = (gate / (1.0 + jnp.exp(-gate)) * up).astype(BF16)
    loads[2].wait()
    scatter(w, dev_at, sub, hid, wd, PB, SB, RB, FB, G1, G3, HB, JB)
    out_ref[...] = (mid_ref[...] + jnp.concatenate([PB[0, 0, 0, 0], PB[0, 0, 0, 1]], axis=1).astype(F32)).astype(BF16)
    w.drain()


def scatter(w, dev_at, sub, hid, wd, PB, SB, RB, FB, G1, G3, HB, JB):
    def blocks(p, c3, target, core, extra):
        dims, h, (r0, r1), _ = PARTS[p]

        @pl.loop(0, 16)
        def _(i):
            r = [None] * 3
            r[dims[0]], r[dims[1]], r[dims[2]] = i // 4, i % 4, c3
            rx, ry, rz = r
            lhs = hid[lax.rem(rx, 2), r0:r1]
            col = dev_at(rx, ry, rz) * 512 + core * 256
            for hh in (0, 1) if p == 2 else (h,):
                part = jnp.dot(lhs, wd[:, pl.ds(pl.multiple_of(col + hh * 128, 128), 128)], preferred_element_type=F32)
                if extra is not None:
                    part = part + extra[rx, ry, rz, hh, r0:r1].astype(F32)
                target[rx, ry, rz, hh, r0:r1] = part.astype(BF16)

    def add(target, sources, p, count, where, half=None):
        _, h, (r0, r1), halves = PARTS[p]
        if half is not None:
            h, (r0, r1) = halves[half]
        hs = (0, 1) if isinstance(h, slice) else (h,)

        def one(i):
            t, ss = where(i)
            for hh in hs:
                total = target[tuple(t) + (hh, slice(r0, r1))].astype(F32)
                for source, s in zip(sources, ss):
                    total = total + source[tuple(s) + (hh, slice(r0, r1))].astype(F32)
                target[tuple(t) + (hh, slice(r0, r1))] = total.astype(BF16)

        if count == 1:
            one(0)
        else:
            pl.loop(0, count)(one)

    def cell(c, i):
        return {"0": (0, 0), "1": (i + 1, 0), "2": (0, i + 1), "3": (i // 3 + 1, i % 3 + 1)}[c]

    count = {"0": 1, "1": 3, "2": 3, "3": 9}

    def spot(p, a, b, c):
        dims = PARTS[p][0]
        r = [None] * 3
        r[dims[0]], r[dims[1]], r[dims[2]] = a, b, c
        return tuple(r)

    order = (2, 1, 3, 0)
    full = slice(0, 4)
    swap = {}
    for c3 in order:
        for p in range(3):
            blocks(p, c3, SB, 1 - sub, None)
            swap[p, c3] = w.post(block(SB, p, full, full, c3), block(RB, p, full, full, c3), None, 0)
    first, second = {}, {}
    for c3 in order:
        for p in range(3):
            d3 = PARTS[p][0][2]
            swap[p, c3].wait_recv()
            blocks(p, c3, PB, sub, RB)
            if c3 == 2:
                for c in "3210":
                    a, b = CHUNKS[c]
                    first[p, c] = [
                        w.post(block(PB, p, a, b, 2, half=0), flat(FB, p, lay(p, a, b), 0), d3, 1),
                        w.post(block(PB, p, a, b, 2, half=1), flat(FB, p, lay(p, a, b), 1), d3, 3),
                    ]
    for c in "3210":
        a, b = CHUNKS[c]
        for p in range(3):
            d3 = PARTS[p][0][2]
            for q, c3 in ((0, 1), (1, 3)):
                first[p, c][q].wait_recv()
                add(PB, (FB,), p, count[c], lambda i: (spot(p, *cell(c, i), c3), (lay(p, *cell(c, i)),)), half=q)
            second[p, c] = [
                w.post(block(PB, p, a, b, 1), flat(G1, p, lay(p, a, b)), d3, 1),
                w.post(block(PB, p, a, b, 3), flat(G3, p, lay(p, a, b)), d3, 3),
            ]
    third, fourth = {}, {}
    for c in "3210":
        for p in range(3):
            d2 = PARTS[p][0][1]
            for copy in second[p, c]:
                copy.wait_recv()
            add(PB, (G1, G3), p, count[c], lambda i: (spot(p, *cell(c, i), 0), (lay(p, *cell(c, i)),) * 2))
            if c in "32":
                a = CHUNKS[c][0]
                third[p, c] = [
                    w.post(block(PB, p, a, k, 0), flat(HB, p, (k - 1, a)), d2, k) for k in (1, 3, 2)
                ]
    for c, a in (("3", slice(1, 4)), ("2", 0)):
        for p in range(3):
            d1 = PARTS[p][0][0]
            for copy in third[p, c]:
                copy.wait_recv()
            n, base = (3, 1) if c == "3" else (1, 0)
            add(PB, (HB,) * 3, p, n, lambda i: (spot(p, i + base, 0, 0), tuple((k, i + base) for k in range(3))))
            if c == "3":
                fourth[p] = [w.post(block(PB, p, k, 0, 0), flat(JB, p, (k - 1,)), d1, k) for k in (1, 3, 2)]
    for p in range(3):
        for copy in fourth[p]:
            copy.wait_recv()
        add(PB, (JB,) * 3, p, 1, lambda i: (spot(p, 0, 0, 0), tuple((k,) for k in range(3))))


def ffn(mid, gain, wg, wu, wd):
    hbm = pl.BlockSpec(memory_space=pl.ANY)
    vmem = pl.BlockSpec(memory_space=pltpu.VMEM)
    grid = (4, 4, 4)
    tail = (2, ROWS, 128)
    return pl.pallas_call(
        ffn_kernel,
        out_shape=jax.ShapeDtypeStruct((ROWS, 256), BF16),
        in_specs=[vmem, vmem, hbm, hbm, hbm],
        out_specs=vmem,
        scratch_shapes=[
            pltpu.VMEM(grid + (2,) + tail, BF16),
            pltpu.VMEM(grid + tail, BF16),
            pltpu.VMEM(grid + tail, BF16),
            pltpu.VMEM(grid + tail, BF16),
            pltpu.VMEM((4, 4) + tail, BF16),
            pltpu.VMEM((4, 4) + tail, BF16),
            pltpu.VMEM((4, 4) + tail, BF16),
            pltpu.VMEM((3, 4) + tail, BF16),
            pltpu.VMEM((3,) + tail, BF16),
            pltpu.VMEM((5, 8, 256), F32),
            pltpu.VMEM((13, 8, 256), F32),
            pltpu.VMEM((HID, D), BF16),
            pltpu.VMEM((HID, D), BF16),
            pltpu.VMEM((HID, D), BF16),
            pltpu.VMEM((2, 2 * ROWS, HID), F32),
            pltpu.VMEM((2, ROWS, HID), BF16),
            pltpu.SemaphoreType.DMA((3,)),
            pltpu.SemaphoreType.DMA((200,)),
            pltpu.SemaphoreType.DMA((200,)),
        ],
        compiler_params=pltpu.CompilerParams(
            collective_id=1, has_side_effects=True, vmem_limit_bytes=60 * 2**20
        ),
        name="ffn",
    )(mid, gain, wg, wu, wd)


def attend(queries, new_keys, new_values, key_cache, value_cache, lengths):
    row_count = queries.shape[0]
    local_kv = new_keys.shape[1] // HEAD_DIM
    per_group = queries.shape[1] // new_keys.shape[1]
    key_span = key_cache.shape[1]
    rescale_factor = 1.0 / HEAD_DIM**0.5
    query_head_rows = queries.reshape(row_count, local_kv, per_group, HEAD_DIM)
    keys_local = key_cache.reshape(row_count, key_span, local_kv, HEAD_DIM)
    values_local = value_cache.reshape(row_count, key_span, local_kv, HEAD_DIM)
    new_key_shard = new_keys.reshape(row_count, local_kv, HEAD_DIM)
    newv_local = new_values.reshape(row_count, local_kv, HEAD_DIM)
    attention_scores = (
        jnp.einsum(
            "bkgd,blkd->bkgl", query_head_rows, keys_local, preferred_element_type=jnp.float32
        )
        * rescale_factor
    )
    self_key_score = (
        jnp.einsum(
            "uyvz,uyz->uyv", query_head_rows, new_key_shard, preferred_element_type=jnp.float32
        )
        * rescale_factor
    )
    valid = (jnp.arange(key_span, dtype=jnp.int32)[None, :] < lengths[:, None])[:, None, None, :]
    masked = jnp.where(valid, attention_scores, jnp.float32(-1e30))
    top_score = jnp.maximum(jnp.max(masked, axis=3), self_key_score)
    weights = jnp.where(valid, jnp.exp(masked - top_score[..., None]), jnp.float32(0.0))
    own_weight = jnp.exp(self_key_score - top_score)
    total = jnp.sum(weights, axis=3) + own_weight
    probs = (weights / total[..., None]).astype(jnp.bfloat16)
    own_probs = (own_weight / total).astype(jnp.bfloat16)
    context = jnp.einsum("bkgl,blkd->bkgd", probs, values_local, preferred_element_type=jnp.float32)
    context = (
        context
        + own_probs.astype(jnp.float32)[..., None] * newv_local.astype(jnp.float32)[:, :, None, :]
    )
    return context.astype(jnp.bfloat16).reshape(row_count, local_kv * per_group * HEAD_DIM)


def shards(
    queries,
    new_keys,
    new_values,
    key_cache,
    value_cache,
    lengths,
    residual,
    o_weight,
    norm_gain,
    w_gate,
    w_up,
    w_down,
):
    context = attend(queries, new_keys, new_values, key_cache, value_cache, lengths)
    partial_out = jnp.dot(
        lax.all_gather(context, "dev", axis=0, tiled=True),
        o_weight,
        preferred_element_type=jnp.float32,
    )
    attention = lax.psum_scatter(
        partial_out.astype(jnp.bfloat16), "sub", scatter_dimension=1, tiled=True
    ).astype(jnp.float32)
    middle_hidden = residual.astype(jnp.float32) + attention
    return ffn(middle_hidden, norm_gain[None, :], w_gate, w_up, w_down)


def solution(mesh):
    placed = (
        P(("grp", "dev"), "sub"),
        P(("grp", "dev"), "sub"),
        P(("grp", "dev"), "sub"),
        P(("grp", "dev"), None, "sub"),
        P(("grp", "dev"), None, "sub"),
        P(("grp", "dev")),
        P("grp", ("dev", "sub")),
        P("sub", "dev"),
        P(("dev", "sub")),
        P(("grp", "dev", "sub"), None),
        P(("grp", "dev", "sub"), None),
        P(("grp", "dev", "sub"), None),
    )
    return jax.shard_map(
        shards, mesh=mesh, in_specs=placed, out_specs=P("grp", ("dev", "sub")), check_vma=False
    )
```

```python
import functools

import jax
import jax.numpy as jnp
from jax import lax
from jax.experimental import pallas as pl
from jax.experimental.pallas import tpu as pltpu
from jax.sharding import PartitionSpec as P

D = 16384
HEAD_DIM = 128
MESH = pl.DeviceIdType.MESH
F32, BF16 = jnp.float32, jnp.bfloat16
ROWS, HID, CACHE = 160, 208, 384
CHUNKS = {
    "0": (0, 0), "1": (slice(1, 4), 0), "2": (0, slice(1, 4)),
    "3": (slice(1, 4), 1), "4": (slice(1, 4), 2), "5": (slice(1, 4), 3),
}
PARTS = (
    ((0, 1, 2), 0, (0, 112), ((0, (0, 64)), (0, (64, 112)))),
    ((1, 2, 0), 1, (0, 112), ((1, (0, 64)), (1, (64, 112)))),
    ((2, 0, 1), slice(0, 2), (112, 160), ((0, (112, 160)), (1, (112, 160)))),
)


def place():
    grp, dev, sub = lax.axis_index("grp"), lax.axis_index("dev"), lax.axis_index("sub")
    return [(dev // 16) * 2 + grp, dev % 4, (dev // 4) % 4], sub


def device(at, sub):
    x, y, z = at
    return (lax.rem(x, 2), (x // 2) * 16 + z * 4 + y, sub)


def shifted(at, dim, by):
    at = list(at)
    at[dim] = lax.rem(at[dim] + by, 4)
    return at


class Wires:
    def __init__(self, at, sub, send, recv):
        self.at, self.sub, self.send, self.recv, self.n = at, sub, send, recv, 0
        self.started = []

    def post(self, src, dst, dim, by):
        if dim is None:
            to = device(self.at, 1 - self.sub)
        else:
            to = device(shifted(self.at, dim, by), self.sub)
        copy = pltpu.make_async_remote_copy(
            src_ref=src, dst_ref=dst, send_sem=self.send.at[self.n], recv_sem=self.recv.at[self.n],
            device_id=to, device_id_type=MESH,
        )
        copy.start()
        self.n += 1
        self.started.append(copy)
        return copy

    def drain(self):
        for copy in self.started:
            copy.wait_send()
        self.started = []


def block(buf, part, a, b, c, tail=(), half=None):
    dims, h, rows, halves = PARTS[part]
    if half is not None:
        h, rows = halves[half]
    idx = [None] * 3
    idx[dims[0]], idx[dims[1]], idx[dims[2]] = a, b, c
    return buf.at[tuple(idx) + tuple(tail) + (h, slice(*rows), slice(None))]


def lay(part, a, b):
    return (b, a) if part == 2 else (a, b)


def flat(buf, part, lead, half=None):
    _, h, rows, halves = PARTS[part]
    if half is not None:
        h, rows = halves[half]
    return buf.at[tuple(lead) + (h, slice(*rows), slice(None))]


def gather(w, XB, sq, ready):
    m1, m2a, m2b, m3, fwd = {}, {}, {}, {}, {}
    own = lambda p: block(XB, p, 0, 0, 0, (0,))
    xb = lambda p, a, b, c, half=None, s=0: block(XB, p, a, b, c, (s,), half)
    d2d = []

    def plane(p, c, up=True):
        a, b = CHUNKS[c]
        d3 = PARTS[p][0][2]
        m3[p, c] = [
            w.post(xb(p, a, b, 0), xb(p, a, b, 3), d3, 1),
            w.post(xb(p, a, b, 0), xb(p, a, b, 1), d3, 3),
        ]

    def onward(p, c):
        a, b = CHUNKS[c]
        d3 = PARTS[p][0][2]
        for copy in m3[p, c]:
            copy.wait_recv()
        fwd[p, c] = [
            w.post(xb(p, a, b, 3, 0), xb(p, a, b, 2, 0), d3, 1),
            w.post(xb(p, a, b, 1, 1), xb(p, a, b, 2, 1), d3, 3),
        ]

    def across(p, a, b, c):
        d2d.append(w.post(xb(p, a, b, c), xb(p, a, b, c, s=1), None, 0))

    for p in range(3):
        d1 = PARTS[p][0][0]
        m1[p] = [w.post(own(p), xb(p, 4 - k, 0, 0), d1, k) for k in (1, 3, 2)]
    for p in range(3):
        d2 = PARTS[p][0][1]
        m2a[p] = [w.post(own(p), xb(p, 0, 4 - k, 0), d2, k) for k in (1, 3, 2)]
    for p in range(3):
        plane(p, "0")
    sq(0)
    for p in range(3):
        d2 = PARTS[p][0][1]
        for copy in m1[p]:
            copy.wait_recv()
        m2b[p] = [w.post(xb(p, slice(1, 4), 0, 0), xb(p, slice(1, 4), 4 - k, 0), d2, k) for k in (1, 3, 2)]
        plane(p, "1")
        across(p, slice(0, 4), 0, 0)
    for p in range(3):
        for copy in m2a[p]:
            copy.wait_recv()
        plane(p, "2")
    sq(1)
    for p in range(3):
        onward(p, "0")
    for i, c in enumerate("534"):
        for p in range(3):
            m2b[p][i].wait_recv()
            plane(p, c)
        if i == 0:
            for p in range(3):
                onward(p, "1")
    sq(2)
    for p in range(3):
        across(p, slice(0, 4), slice(1, 4), 0)
        onward(p, "2")
    ready(0)
    sq(3)
    for c in "534":
        for p in range(3):
            onward(p, c)
    for p in range(3):
        across(p, slice(0, 4), slice(0, 4), 1)
        across(p, slice(0, 4), slice(0, 4), 3)
    sq(4)
    ready(1)
    for chunks, r2 in (("01", 0), ("25", 3), ("3", 1), ("4", 2)):
        for p in range(3):
            for c in chunks:
                for copy in fwd[p, c]:
                    copy.wait_recv()
            across(p, slice(0, 4), r2, 2)
    for copy in d2d:
        copy.wait_recv()
    ready(2)


def attention(q_ref, nk_ref, nv_ref, kc, vc, len_ref, qs, CB):
    for h in range(32):
        qs[pl.ds(h, 5, stride=32), :] = q_ref[:, h * 128:(h + 1) * 128].astype(F32)
    span = lax.broadcasted_iota(jnp.int32, (16, CACHE), 1)
    scale = 1.0 / HEAD_DIM**0.5
    for b in range(5):
        for g in range(2):
            cols = slice(g * 128, (g + 1) * 128)
            q = qs[b * 32 + g * 16:b * 32 + (g + 1) * 16]
            scores = lax.dot_general(
                q.astype(BF16), kc[b, :, cols], (((1,), (1,)), ((), ())), preferred_element_type=F32
            ) * scale
            own = jnp.sum(q * nk_ref[b:b + 1, cols].astype(F32), axis=1, keepdims=True) * scale
            valid = span < len_ref[b]
            masked = jnp.where(valid, scores, -1e30)
            top = jnp.maximum(jnp.max(masked, axis=1, keepdims=True), own)
            weights = jnp.where(valid, jnp.exp(masked - top), 0.0)
            own = jnp.exp(own - top)
            total = jnp.sum(weights, axis=1, keepdims=True) + own
            probs = (weights / total).astype(BF16)
            own = (own / total).astype(BF16).astype(F32)
            context = jnp.dot(probs, vc[b, :, cols], preferred_element_type=F32)
            context = context + own * nv_ref[b:b + 1, cols].astype(F32)
            CB[0, 0, 0, b * 32 + g * 16:b * 32 + (g + 1) * 16] = context.astype(BF16)


def project(w, at, sub, CB, LH, wo, wo_load, half_out, half_in):
    x0, y0, z0 = at

    def part(q, rx, ry, rz):
        return CB.at[rx, ry, rz, q * 80:(q + 1) * 80]

    def cut(q, rx, a, b):
        return part(q, rx, *((b, a) if q == 0 else (a, b)))

    dims = ((2, 1), (1, 2))
    turns = (1, 3, 2)
    both = slice(0, 2)

    def settle(rx, ry, rz):
        dev = (lax.rem(x0 + 2 * rx, 4) // 2) * 16 + lax.rem(z0 + rz, 4) * 4 + lax.rem(y0 + ry, 4)
        for b in range(5):
            LH[pl.ds(dev * 5 + b, 32, stride=ROWS), :] = CB[rx, ry, rz, b * 32:(b + 1) * 32].astype(F32)

    hop = [w.post(part(q, 0, 0, 0), part(q, 1, 0, 0), 0, 2) for q in range(2)]
    near = [[w.post(cut(q, 0, 0, 0), cut(q, 0, 4 - k, 0), dims[q][0], k) for k in turns] for q in range(2)]
    settle(0, 0, 0)
    far, plane = [], [[], []]
    for q in range(2):
        hop[q].wait_recv()
        far.append([w.post(cut(q, 1, 0, 0), cut(q, 1, 4 - k, 0), dims[q][0], k) for k in turns])
        plane[q] += [w.post(cut(q, both, 0, 0), cut(q, both, 0, 4 - k), dims[q][1], k) for k in turns]
    settle(1, 0, 0)
    for i in range(3):
        r = 4 - turns[i]
        for q in range(2):
            near[q][i].wait_recv()
            far[q][i].wait_recv()
            plane[q] += [w.post(cut(q, both, r, 0), cut(q, both, r, 4 - k), dims[q][1], k) for k in turns]
    for q in range(2):
        for copy in plane[q]:
            copy.wait_recv()

    @pl.loop(0, 30)
    def _(i):
        i = i + 1 + i // 15
        settle(i // 16, (i // 4) % 4, i % 4)

    wo_load.wait()

    def half(core):
        total = jnp.zeros((ROWS, 256), F32)
        col = pl.multiple_of(core * 256, 256)

        def step(i, total):
            lhs = jnp.concatenate(
                [LH[pl.ds(pl.multiple_of((i * 8 + j) * ROWS, ROWS), ROWS), :].astype(BF16) for j in range(8)], axis=1
            )
            rhs = wo[pl.ds(pl.multiple_of(i * 1024, 1024), 1024), pl.ds(col, 256)]
            return total + jnp.dot(lhs, rhs, preferred_element_type=F32)

        return lax.fori_loop(0, 4, step, total)

    half_out[...] = half(1 - sub).astype(BF16)
    swap = w.post(half_out, half_in, None, 0)
    mine = half(sub)
    swap.wait_recv()
    return mine + half_in[...].astype(F32)


def ffn_kernel(q_ref, nk_ref, nv_ref, kc_hbm, vc_hbm, len_ref, res_ref, wo_hbm, gain_ref, wg_hbm, wu_hbm, wd_hbm, out_ref,
               kc, vc, wo, qs, CB, LH, half_out, half_in, mid_ref,
               XB, PB, SB, RB, FB, G1, G3, HB, JB, sqs, sqr, wg, wu, wd, acc, hid, wsem, send, recv):
    at, sub = place()
    x0, y0, z0 = at
    grp = lax.rem(x0, 2)
    w = Wires(at, sub, send, recv)
    pairs = ((wg_hbm, wg), (wu_hbm, wu), (wd_hbm, wd), (kc_hbm, kc), (vc_hbm, vc), (wo_hbm, wo))
    loads = [pltpu.make_async_copy(a, b, wsem.at[i]) for i, (a, b) in enumerate(pairs)]
    loads = [loads[i] for i in (3, 4, 5, 0, 1, 2)]
    for load in loads:
        load.start()
    barrier = pltpu.get_barrier_semaphore()
    for dim in range(3):
        for by in (1, 2, 3):
            pl.semaphore_signal(barrier, inc=1, device_id=device(shifted(at, dim, by), sub), device_id_type=MESH)
    pl.semaphore_signal(barrier, inc=1, device_id=device(at, 1 - sub), device_id_type=MESH)

    loads[0].wait()
    loads[1].wait()
    attention(q_ref, nk_ref, nv_ref, kc, vc, len_ref, qs, CB)
    pl.semaphore_wait(barrier, 10)
    mid = project(w, at, sub, CB, LH, wo, loads[2], half_out, half_in) + res_ref[...].astype(F32)
    mid_ref[...] = mid
    loads = loads[3:]

    rows = (mid * gain_ref[...].astype(F32)).astype(BF16)
    XB[0, 0, 0, 0, 0] = rows[:, :128]
    XB[0, 0, 0, 0, 1] = rows[:, 128:]
    eye = lax.broadcasted_iota(jnp.int32, (ROWS, 256), 0) == lax.broadcasted_iota(jnp.int32, (ROWS, 256), 1)
    column = jnp.sum(mid * mid, axis=1, keepdims=True)
    sqs[0] = jnp.broadcast_to(jnp.sum(jnp.where(eye, column, 0.0), axis=0, keepdims=True), (8, 256))

    sq_copies = {}

    def sq(step):
        if step > 0:
            total = sqs[step - 1]
            for i, copy in enumerate(sq_copies[step - 1]):
                copy.wait_recv()
                total = total + sqr[(step - 1) * 3 + i]
            sqs[step] = total
        if step == 0:
            sq_copies[0] = [w.post(sqs.at[0], sqr.at[0], None, 0)]
        elif step == 1:
            sq_copies[1] = [w.post(sqs.at[1], sqr.at[3 + i], 1, k) for i, k in enumerate((1, 3, 2))]
        elif step == 2:
            sq_copies[2] = [w.post(sqs.at[2], sqr.at[6 + i], 2, k) for i, k in enumerate((1, 3, 2))]
        elif step == 3:
            sq_copies[3] = [w.post(sqs.at[3], sqr.at[9], 0, 2)]
        else:
            sq_copies[4] = [w.post(sqs.at[4], sqr.at[12], 0, 1)]

    def dev_at(rx, ry, rz):
        return (lax.rem(x0 + rx, 4) // 2) * 16 + lax.rem(z0 + rz, 4) * 4 + lax.rem(y0 + ry, 4)

    def ready(step):
        if step != 2:
            return
        loads[0].wait()
        loads[1].wait()
        acc[...] = jnp.zeros_like(acc)

        @pl.loop(0, 8)
        def _(i):
            rx, ry = (i // 4) * 2, i % 4
            other = lax.rem(rx + 5 - 2 * grp, 4)
            ks = [pl.multiple_of(dev_at(rx, ry, rz) * 512, 512) for rz in range(4)]
            lhs = jnp.concatenate(
                [
                    jnp.concatenate([XB[q, ry, rz, s, h] for rz in range(4) for s in (sub, 1 - sub) for h in (0, 1)], axis=1)
                    for q in (rx, other)
                ],
                axis=0,
            )
            for j, weight in enumerate((wg, wu)):
                rhs = jnp.concatenate([weight[:, pl.ds(k, 512)] for k in ks], axis=1)
                acc[j] += lax.dot_general(lhs, rhs, (((1,), (1,)), ((), ())), preferred_element_type=F32)

    gather(w, XB, sq, ready)

    sq_copies[4][0].wait_recv()
    for i, sums in enumerate((sqs[4], sqr[12])):
        inv_row = lax.rsqrt(sums[0:1] / D + 1e-05)
        inv = jnp.sum(jnp.where(eye, inv_row, 0.0), axis=1, keepdims=True)
        gate = acc[0, i * ROWS:(i + 1) * ROWS] * inv
        up = acc[1, i * ROWS:(i + 1) * ROWS] * inv
        hid[i] = (gate / (1.0 + jnp.exp(-gate)) * up).astype(BF16)
    loads[2].wait()
    scatter(w, dev_at, sub, hid, wd, PB, SB, RB, FB, G1, G3, HB, JB)
    out_ref[...] = (mid_ref[...] + jnp.concatenate([PB[0, 0, 0, 0], PB[0, 0, 0, 1]], axis=1).astype(F32)).astype(BF16)
    w.drain()


def scatter(w, dev_at, sub, hid, wd, PB, SB, RB, FB, G1, G3, HB, JB):
    def blocks(count, where, target, core, extra):
        @pl.loop(0, count, unroll=4 if count % 4 == 0 else 3)
        def _(i):
            rx, ry, rz = where(i)
            col = pl.multiple_of(dev_at(rx, ry, rz) * 512 + core * 256, 256)
            part = jnp.dot(hid[lax.rem(rx, 2)], wd[:, pl.ds(col, 256)], preferred_element_type=F32)
            for h in (0, 1):
                one = part[:, h * 128:(h + 1) * 128]
                if extra is not None:
                    one = one + extra[rx, ry, rz, h].astype(F32)
                target[rx, ry, rz, h] = one.astype(BF16)

    def add(target, sources, p, count, where, half=None):
        _, h, (r0, r1), halves = PARTS[p]
        if half is not None:
            h, (r0, r1) = halves[half]
        hs = (0, 1) if isinstance(h, slice) else (h,)

        def one(i):
            t, ss = where(i)
            for hh in hs:
                total = target[tuple(t) + (hh, slice(r0, r1))].astype(F32)
                for source, s in zip(sources, ss):
                    total = total + source[tuple(s) + (hh, slice(r0, r1))].astype(F32)
                target[tuple(t) + (hh, slice(r0, r1))] = total.astype(BF16)

        if count == 1:
            one(0)
        else:
            pl.loop(0, count, unroll=count)(one)

    def cell(c, i):
        return {"0": (0, 0), "1": (i + 1, 0), "2": (0, i + 1), "3": (i + 1, 1), "4": (i + 1, 2), "5": (i + 1, 3)}[c]

    count = {"0": 1, "1": 3, "2": 3, "3": 3, "4": 3, "5": 3}

    def spot(p, a, b, c):
        dims = PARTS[p][0]
        r = [None] * 3
        r[dims[0]], r[dims[1]], r[dims[2]] = a, b, c
        return tuple(r)

    skip = lambda v: v + v // 2
    near = (slice(0, 2), 3)
    sets = (
        (16, lambda i: (2, i // 4, i % 4), [(2, slice(0, 4), slice(0, 4))]),
        (12, lambda i: (skip(i // 4), i % 4, 2), [(a, slice(0, 4), 2) for a in near]),
        (9, lambda i: (skip(i // 3), 2, skip(i % 3)), [(a, 2, c) for a in near for c in near]),
        (27, lambda i: (skip(i // 9), skip((i // 3) % 3), skip(i % 3)), [(a, b, c) for a in near for b in near for c in near]),
    )
    swap = {}

    def far_core(n):
        total, where, slices = sets[n]
        blocks(total, where, SB, 1 - sub, None)
        swap[n] = [w.post(SB.at[idx], RB.at[idx], None, 0) for idx in slices]

    def near_core(n):
        for copy in swap[n]:
            copy.wait_recv()
        total, where, _ = sets[n]
        blocks(total, where, PB, sub, RB)

    first, second, third, fourth = {}, {}, {}, {}
    order = "435210"

    def start(p):
        d3 = PARTS[p][0][2]
        for c in order:
            a, b = CHUNKS[c]
            first[p, c] = [
                w.post(block(PB, p, a, b, 2, half=0), flat(FB, p, lay(p, a, b), 0), d3, 1),
                w.post(block(PB, p, a, b, 2, half=1), flat(FB, p, lay(p, a, b), 1), d3, 3),
            ]

    far_core(0)
    far_core(1)
    near_core(0)
    start(1)
    far_core(2)
    near_core(1)
    start(0)
    near_core(2)
    start(2)
    far_core(3)
    near_core(3)

    def pass_on(c):
        a, b = CHUNKS[c]
        for p in (1, 0, 2):
            d3 = PARTS[p][0][2]
            for q, c3 in ((0, 1), (1, 3)):
                first[p, c][q].wait_recv()
                add(PB, (FB,), p, count[c], lambda i: (spot(p, *cell(c, i), c3), (lay(p, *cell(c, i)),)), half=q)
            second[p, c] = [
                w.post(block(PB, p, a, b, 1), flat(G1, p, lay(p, a, b)), d3, 1),
                w.post(block(PB, p, a, b, 3), flat(G3, p, lay(p, a, b)), d3, 3),
            ]

    def collect(c):
        a, b = CHUNKS[c]
        for p in (1, 0, 2):
            d2 = PARTS[p][0][1]
            for copy in second[p, c]:
                copy.wait_recv()
            add(PB, (G1, G3), p, count[c], lambda i: (spot(p, *cell(c, i), 0), (lay(p, *cell(c, i)),) * 2))
            if c in "345":
                third[p, b] = w.post(block(PB, p, a, b, 0), flat(HB, p, (b - 1, a)), d2, b)
            if c == "2":
                third[p, 0] = [w.post(block(PB, p, 0, k, 0), flat(HB, p, (k - 1, 0)), d2, k) for k in (1, 3, 2)]

    for c in order:
        pass_on(c)
    for c in order:
        collect(c)
    for p in (1, 0, 2):
        d1 = PARTS[p][0][0]
        for k in (2, 1, 3):
            third[p, k].wait_recv()
        add(PB, (HB,) * 3, p, 3, lambda i: (spot(p, i + 1, 0, 0), tuple((k, i + 1) for k in range(3))))
        fourth[p] = [w.post(block(PB, p, k, 0, 0), flat(JB, p, (k - 1,)), d1, k) for k in (1, 3, 2)]
    for p in (1, 0, 2):
        for copy in third[p, 0]:
            copy.wait_recv()
        add(PB, (HB,) * 3, p, 1, lambda i: (spot(p, 0, 0, 0), tuple((k, 0) for k in range(3))))
    for p in (1, 0, 2):
        for copy in fourth[p]:
            copy.wait_recv()
        add(PB, (JB,) * 3, p, 1, lambda i: (spot(p, 0, 0, 0), tuple((k,) for k in range(3))))


def ffn(q, nk, nv, kc, vc, lengths, res, wo, gain, wg, wu, wd):
    hbm = pl.BlockSpec(memory_space=pl.ANY)
    vmem = pl.BlockSpec(memory_space=pltpu.VMEM)
    smem = pl.BlockSpec(memory_space=pltpu.SMEM)
    grid = (4, 4, 4)
    tail = (2, ROWS, 128)
    return pl.pallas_call(
        ffn_kernel,
        out_shape=jax.ShapeDtypeStruct((ROWS, 256), BF16),
        in_specs=[vmem, vmem, vmem, hbm, hbm, smem, vmem, hbm, vmem, hbm, hbm, hbm],
        out_specs=vmem,
        scratch_shapes=[
            pltpu.VMEM((5, CACHE, 256), BF16),
            pltpu.VMEM((5, CACHE, 256), BF16),
            pltpu.VMEM((4096, 512), BF16),
            pltpu.VMEM((ROWS, 128), F32),
            pltpu.VMEM((2, 4, 4, ROWS, 128), BF16),
            pltpu.VMEM((32 * ROWS, 128), F32),
            pltpu.VMEM((ROWS, 256), BF16),
            pltpu.VMEM((ROWS, 256), BF16),
            pltpu.VMEM((ROWS, 256), F32),
            pltpu.VMEM(grid + (2,) + tail, BF16),
            pltpu.VMEM(grid + tail, BF16),
            pltpu.VMEM(grid + tail, BF16),
            pltpu.VMEM(grid + tail, BF16),
            pltpu.VMEM((4, 4) + tail, BF16),
            pltpu.VMEM((4, 4) + tail, BF16),
            pltpu.VMEM((4, 4) + tail, BF16),
            pltpu.VMEM((3, 4) + tail, BF16),
            pltpu.VMEM((3,) + tail, BF16),
            pltpu.VMEM((5, 8, 256), F32),
            pltpu.VMEM((13, 8, 256), F32),
            pltpu.VMEM((HID, D), BF16),
            pltpu.VMEM((HID, D), BF16),
            pltpu.VMEM((HID, D), BF16),
            pltpu.VMEM((2, 2 * ROWS, HID), F32),
            pltpu.VMEM((2, ROWS, HID), BF16),
            pltpu.SemaphoreType.DMA((6,)),
            pltpu.SemaphoreType.DMA((300,)),
            pltpu.SemaphoreType.DMA((300,)),
        ],
        compiler_params=pltpu.CompilerParams(
            collective_id=1, has_side_effects=True, vmem_limit_bytes=62 * 2**20
        ),
        name="ffn",
    )(q, nk, nv, kc, vc, lengths, res, wo, gain, wg, wu, wd)


def shards(
    queries,
    new_keys,
    new_values,
    key_cache,
    value_cache,
    lengths,
    residual,
    o_weight,
    norm_gain,
    w_gate,
    w_up,
    w_down,
):
    return ffn(
        queries, new_keys, new_values, key_cache, value_cache, lengths, residual,
        o_weight, norm_gain[None, :], w_gate, w_up, w_down,
    )


def solution(mesh):
    placed = (
        P(("grp", "dev"), "sub"),
        P(("grp", "dev"), "sub"),
        P(("grp", "dev"), "sub"),
        P(("grp", "dev"), None, "sub"),
        P(("grp", "dev"), None, "sub"),
        P(("grp", "dev")),
        P("grp", ("dev", "sub")),
        P("sub", "dev"),
        P(("dev", "sub")),
        P(("grp", "dev", "sub"), None),
        P(("grp", "dev", "sub"), None),
        P(("grp", "dev", "sub"), None),
    )
    return jax.shard_map(
        shards, mesh=mesh, in_specs=placed, out_specs=P("grp", ("dev", "sub")), check_vma=False
    )
```

```python
import functools

import jax
import jax.numpy as jnp
from jax import lax
from jax.experimental import pallas as pl
from jax.experimental.pallas import tpu as pltpu
from jax.sharding import PartitionSpec as P

D = 16384
HEAD_DIM = 128
MESH = pl.DeviceIdType.MESH
F32, BF16 = jnp.float32, jnp.bfloat16
ROWS, HID, CACHE = 160, 208, 384
CHUNKS = {
    "0": (0, 0), "1": (slice(1, 4), 0), "2": (0, slice(1, 4)),
    "3": (slice(1, 4), 1), "4": (slice(1, 4), 2), "5": (slice(1, 4), 3),
}
FLIP = {"0": 0, "1": 1, "2": 0, "3": 0, "4": 1, "5": 0}
PARTS = (
    ((0, 1, 2), 0, (0, 112), ((0, (0, 64)), (0, (64, 112)))),
    ((1, 2, 0), 1, (0, 112), ((1, (0, 64)), (1, (64, 112)))),
    ((2, 0, 1), slice(0, 2), (112, 160), ((0, (112, 160)), (1, (112, 160)))),
)


def place():
    grp, dev, sub = lax.axis_index("grp"), lax.axis_index("dev"), lax.axis_index("sub")
    return [(dev // 16) * 2 + grp, dev % 4, (dev // 4) % 4], sub


def device(at, sub):
    x, y, z = at
    return (lax.rem(x, 2), (x // 2) * 16 + z * 4 + y, sub)


def shifted(at, dim, by):
    at = list(at)
    at[dim] = lax.rem(at[dim] + by, 4)
    return at


class Wires:
    def __init__(self, at, sub, send, recv):
        self.at, self.sub, self.send, self.recv, self.n = at, sub, send, recv, 0
        self.started = []

    def post(self, src, dst, dim, by):
        if dim is None:
            to = device(self.at, 1 - self.sub)
        else:
            to = device(shifted(self.at, dim, by), self.sub)
        copy = pltpu.make_async_remote_copy(
            src_ref=src, dst_ref=dst, send_sem=self.send.at[self.n], recv_sem=self.recv.at[self.n],
            device_id=to, device_id_type=MESH,
        )
        copy.start()
        self.n += 1
        self.started.append(copy)
        return copy

    def sent(self, copy):
        copy.wait_send()
        self.started = [c for c in self.started if c is not copy]

    def drain(self):
        for copy in self.started:
            copy.wait_send()
        self.started = []


def block(buf, part, a, b, c, tail=(), half=None):
    dims, h, rows, halves = PARTS[part]
    if half is not None:
        h, rows = halves[half]
    idx = [None] * 3
    idx[dims[0]], idx[dims[1]], idx[dims[2]] = a, b, c
    return buf.at[tuple(idx) + tuple(tail) + (h, slice(*rows), slice(None))]


def lay(part, a, b):
    return (b, a) if part == 2 else (a, b)


def flat(buf, part, lead, half=None):
    _, h, rows, halves = PARTS[part]
    if half is not None:
        h, rows = halves[half]
    return buf.at[tuple(lead) + (h, slice(*rows), slice(None))]


def gather(w, XB, sq, ready):
    m1, m2a, m2b, m3, fwd = {}, {}, {}, {}, {}
    own = lambda p: block(XB, p, 0, 0, 0, (0,))
    xb = lambda p, a, b, c, half=None, s=0: block(XB, p, a, b, c, (s,), half)
    d2d = []

    def plane(p, c, up=True):
        a, b = CHUNKS[c]
        d3 = PARTS[p][0][2]
        m3[p, c] = [
            w.post(xb(p, a, b, 0), xb(p, a, b, 3), d3, 1),
            w.post(xb(p, a, b, 0), xb(p, a, b, 1), d3, 3),
        ]

    def onward(p, c):
        a, b = CHUNKS[c]
        d3 = PARTS[p][0][2]
        f = FLIP[c]
        for copy in m3[p, c]:
            copy.wait_recv()
        fwd[p, c] = [
            w.post(xb(p, a, b, 3, f), xb(p, a, b, 2, f), d3, 1),
            w.post(xb(p, a, b, 1, 1 - f), xb(p, a, b, 2, 1 - f), d3, 3),
        ]

    def landed(copies):
        for copy in copies:
            copy.wait_recv()

    def across(p, a, b, c):
        d2d.append(w.post(xb(p, a, b, c), xb(p, a, b, c, s=1), None, 0))

    for p in range(3):
        d1 = PARTS[p][0][0]
        m1[p] = [w.post(own(p), xb(p, 4 - k, 0, 0), d1, k) for k in (1, 3, 2)]
    for p in range(3):
        d2 = PARTS[p][0][1]
        m2a[p] = [w.post(own(p), xb(p, 0, 4 - k, 0), d2, k) for k in (1, 3, 2)]
    for p in range(3):
        plane(p, "0")
    sq(0)
    for p in range(3):
        d2 = PARTS[p][0][1]
        for copy in m1[p]:
            copy.wait_recv()
        m2b[p] = [w.post(xb(p, slice(1, 4), 0, 0), xb(p, slice(1, 4), 4 - k, 0), d2, k) for k in (1, 3, 2)]
    for p in range(3):
        plane(p, "1")
    for p in range(3):
        for copy in m2a[p]:
            copy.wait_recv()
        plane(p, "2")
        across(p, slice(0, 4), 0, 0)
    sq(1)
    for p in range(3):
        onward(p, "0")
    for i, c in enumerate("53"):
        for p in range(3):
            m2b[p][i].wait_recv()
            plane(p, c)
    sq(2)
    for p in range(3):
        m2b[p][2].wait_recv()
        plane(p, "4")
        across(p, slice(0, 4), slice(1, 4), 0)
    for c in "12":
        for p in range(3):
            onward(p, c)
    sq(3)
    for p in range(3):
        onward(p, "5")
    for p in range(3):
        for c in "012":
            for copy in fwd[p, c]:
                copy.wait_recv()
        across(p, slice(0, 4), 0, slice(1, 4))
        across(p, 0, slice(1, 4), slice(1, 4))
    early = list(d2d)
    d2d.clear()
    for p in range(3):
        onward(p, "3")
    for p in range(3):
        onward(p, "4")
        across(p, slice(1, 4), slice(1, 4), 1)
        across(p, slice(1, 4), slice(1, 4), 3)
    sq(4)
    landed(early)
    for step in range(4):
        ready(step)
    landed(d2d)
    ready(4)
    for r2, c in ((3, "5"), (1, "3"), (2, "4")):
        for p in range(3):
            for copy in fwd[p, c]:
                copy.wait_recv()
            across(p, slice(1, 4), r2, 2)
    landed(d2d[6:])
    for step in (5, 6, 7, 8):
        ready(step)


def attention(q_ref, nk_ref, nv_ref, kc, vc, len_ref, qs, CB):
    for h in range(32):
        qs[pl.ds(h, 5, stride=32), :] = q_ref[:, h * 128:(h + 1) * 128].astype(F32)
    span = lax.broadcasted_iota(jnp.int32, (16, CACHE), 1)
    scale = 1.0 / HEAD_DIM**0.5
    for b in range(5):
        for g in range(2):
            cols = slice(g * 128, (g + 1) * 128)
            q = qs[b * 32 + g * 16:b * 32 + (g + 1) * 16]
            scores = lax.dot_general(
                q.astype(BF16), kc[b, :, cols], (((1,), (1,)), ((), ())), preferred_element_type=F32
            ) * scale
            own = jnp.sum(q * nk_ref[b:b + 1, cols].astype(F32), axis=1, keepdims=True) * scale
            valid = span < len_ref[b]
            masked = jnp.where(valid, scores, -1e30)
            top = jnp.maximum(jnp.max(masked, axis=1, keepdims=True), own)
            weights = jnp.where(valid, jnp.exp(masked - top), 0.0)
            own = jnp.exp(own - top)
            total = jnp.sum(weights, axis=1, keepdims=True) + own
            probs = (weights / total).astype(BF16)
            own = (own / total).astype(BF16).astype(F32)
            context = jnp.dot(probs, vc[b, :, cols], preferred_element_type=F32)
            context = context + own * nv_ref[b:b + 1, cols].astype(F32)
            CB[0, 0, 0, b * 32 + g * 16:b * 32 + (g + 1) * 16] = context.astype(BF16)


def project(w, at, sub, CB, LH, wo, wo_load, half_out, half_in, mid_ref):
    x0, y0, z0 = at

    def part(q, rx, ry, rz):
        return CB.at[rx, ry, rz, q * 80:(q + 1) * 80]

    def cut(q, rx, a, b):
        return part(q, rx, *((b, a) if q == 0 else (a, b)))

    dims = ((2, 1), (1, 2))
    turns = (1, 3, 2)
    both = slice(0, 2)

    def settle(rx, ry, rz):
        dev = (lax.rem(x0 + 2 * rx, 4) // 2) * 16 + lax.rem(z0 + rz, 4) * 4 + lax.rem(y0 + ry, 4)
        for b in range(5):
            LH[pl.ds(dev * 5 + b, 32, stride=ROWS), :] = CB[rx, ry, rz, b * 32:(b + 1) * 32].astype(F32)

    planes = [[], []]

    def plane(q, rx, r):
        planes[q] += [w.post(cut(q, rx, r, 0), cut(q, rx, r, 4 - k), dims[q][1], k) for k in turns]

    hop = [w.post(part(q, 0, 0, 0), part(q, 1, 0, 0), 0, 2) for q in range(2)]
    near = [[w.post(cut(q, 0, 0, 0), cut(q, 0, 4 - k, 0), dims[q][0], k) for k in turns] for q in range(2)]
    for q in range(2):
        plane(q, 0, 0)
    settle(0, 0, 0)
    far = []
    for q in range(2):
        hop[q].wait_recv()
        far.append([w.post(cut(q, 1, 0, 0), cut(q, 1, 4 - k, 0), dims[q][0], k) for k in turns])
    for i in range(3):
        for q in range(2):
            near[q][i].wait_recv()
            plane(q, 0, 4 - turns[i])
    for q in range(2):
        plane(q, 1, 0)
    settle(1, 0, 0)
    for i in range(3):
        for q in range(2):
            far[q][i].wait_recv()
            plane(q, 1, 4 - turns[i])
    for q in range(2):
        for copy in planes[q]:
            copy.wait_recv()

    @pl.loop(0, 30)
    def _(i):
        i = i + 1 + i // 15
        settle(i // 16, (i // 4) % 4, i % 4)

    wo_load.wait()

    def step(i, total):
        lhs = jnp.concatenate(
            [LH[pl.ds(pl.multiple_of((i * 8 + j) * ROWS, ROWS), ROWS), :].astype(BF16) for j in range(8)], axis=1
        )
        rhs = wo[pl.ds(pl.multiple_of(i * 1024, 1024), 1024), :]
        return total + jnp.dot(lhs, rhs, preferred_element_type=F32)

    total = lax.fori_loop(0, 4, step, jnp.zeros((ROWS, 512), F32))
    for core in range(2):
        half_out[core] = total[:, core * 256:(core + 1) * 256].astype(BF16)
        mid_ref[core] = total[:, core * 256:(core + 1) * 256]
    swap = w.post(half_out.at[1 - sub], half_in, None, 0)
    mine = mid_ref[sub]
    swap.wait_recv()
    return mine + half_in[...].astype(F32)


def ffn_kernel(q_ref, nk_ref, nv_ref, kc_hbm, vc_hbm, len_ref, res_ref, wo_hbm, gain_ref, wg_hbm, wu_hbm, wd_hbm, out_ref,
               kc, vc, wo, qs, CB, LH, half_out, half_in, mid_ref,
               XB, PB, SB, RB, FB, G1, G3, HB, JB, sqs, sqr, wg, wu, wd, acc, hid, wsem, send, recv):
    at, sub = place()
    x0, y0, z0 = at
    grp = lax.rem(x0, 2)
    w = Wires(at, sub, send, recv)
    pairs = ((wg_hbm, wg), (wu_hbm, wu), (wd_hbm, wd), (kc_hbm, kc), (vc_hbm, vc), (wo_hbm, wo))
    loads = [pltpu.make_async_copy(a, b, wsem.at[i]) for i, (a, b) in enumerate(pairs)]
    loads = [loads[i] for i in (3, 4, 5, 0, 1, 2)]
    for load in loads:
        load.start()
    barrier = pltpu.get_barrier_semaphore()
    for dim in range(3):
        for by in (1, 2, 3):
            pl.semaphore_signal(barrier, inc=1, device_id=device(shifted(at, dim, by), sub), device_id_type=MESH)
    pl.semaphore_signal(barrier, inc=1, device_id=device(at, 1 - sub), device_id_type=MESH)

    loads[0].wait()
    loads[1].wait()
    attention(q_ref, nk_ref, nv_ref, kc, vc, len_ref, qs, CB)
    pl.semaphore_wait(barrier, 10)
    mid = project(w, at, sub, CB, LH, wo, loads[2], half_out, half_in, mid_ref) + res_ref[...].astype(F32)
    mid_ref[0] = mid
    loads = loads[3:]

    rows = (mid * gain_ref[...].astype(F32)[None, :]).astype(BF16)
    XB[0, 0, 0, 0, 0] = rows[:, :128]
    XB[0, 0, 0, 0, 1] = rows[:, 128:]
    eye = lax.broadcasted_iota(jnp.int32, (ROWS, 256), 0) == lax.broadcasted_iota(jnp.int32, (ROWS, 256), 1)
    column = jnp.sum(mid * mid, axis=1, keepdims=True)
    sqs[0] = jnp.broadcast_to(jnp.sum(jnp.where(eye, column, 0.0), axis=0, keepdims=True), (8, 256))

    sq_copies = {}

    def sq(step):
        if step > 0:
            total = sqs[step - 1]
            for i, copy in enumerate(sq_copies[step - 1]):
                copy.wait_recv()
                total = total + sqr[(step - 1) * 3 + i]
            sqs[step] = total
        if step == 0:
            sq_copies[0] = [w.post(sqs.at[0], sqr.at[0], None, 0)]
        elif step == 1:
            sq_copies[1] = [w.post(sqs.at[1], sqr.at[3 + i], 1, k) for i, k in enumerate((1, 3, 2))]
        elif step == 2:
            sq_copies[2] = [w.post(sqs.at[2], sqr.at[6 + i], 2, k) for i, k in enumerate((1, 3, 2))]
        elif step == 3:
            sq_copies[3] = [w.post(sqs.at[3], sqr.at[9], 0, 2)]
        else:
            sq_copies[4] = [w.post(sqs.at[4], sqr.at[12], 0, 1)]

    def dev_at(rx, ry, rz):
        return (lax.rem(x0 + rx, 4) // 2) * 16 + lax.rem(z0 + rz, 4) * 4 + lax.rem(y0 + ry, 4)

    corner = [(r, 0, rz) for r in (0, 2) for rz in range(4)] + [(r, ry, 0) for r in (0, 2) for ry in (1, 2, 3)]
    odd = [(0, ry, rz) for ry in (1, 3) for rz in (1, 3)]
    last = [(r, ry, rz) for r in (0, 2) for ry in (1, 2, 3) for rz in (1, 2, 3) if r or ry == 2 or rz == 2]
    batches = {0: corner[0:4], 1: corner[4:8], 2: corner[8:11], 3: corner[11:14], 4: odd,
               5: last[0:4], 6: last[4:8], 7: last[8:11], 8: last[11:14]}

    def ready(step):
        if step == 0:
            loads[0].wait()
            loads[1].wait()
        pairs = [(rx, lax.rem(rx + 5 - 2 * grp, 4), ry, rz) for rx, ry, rz in batches[step]]
        ks = [pl.multiple_of(dev_at(rx, ry, rz) * 512, 512) for rx, _, ry, rz in pairs]
        lhs = jnp.concatenate(
            [
                jnp.concatenate(
                    [XB[pair[q], pair[2], pair[3], s, h] for pair in pairs for s in (sub, 1 - sub) for h in (0, 1)], axis=1
                )
                for q in (0, 1)
            ],
            axis=0,
        )
        for j, weight in enumerate((wg, wu)):
            rhs = jnp.concatenate([weight[:, pl.ds(k, 512)] for k in ks], axis=1)
            part = lax.dot_general(lhs, rhs, (((1,), (1,)), ((), ())), preferred_element_type=F32)
            acc[j] = part if step == 0 else acc[j] + part

    gather(w, XB, sq, ready)

    sq_copies[4][0].wait_recv()
    for i, sums in enumerate((sqs[4], sqr[12])):
        inv_row = lax.rsqrt(sums[0:1] / D + 1e-05)
        inv = jnp.sum(jnp.where(eye, inv_row, 0.0), axis=1, keepdims=True)
        gate = acc[0, i * ROWS:(i + 1) * ROWS] * inv
        up = acc[1, i * ROWS:(i + 1) * ROWS] * inv
        hid[i] = (gate / (1.0 + jnp.exp(-gate)) * up).astype(BF16)
    loads[2].wait()
    scatter(w, dev_at, sub, hid, wd, PB, SB, RB, FB, G1, G3, HB, JB)
    out_ref[...] = (mid_ref[0] + jnp.concatenate([PB[0, 0, 0, 0], PB[0, 0, 0, 1]], axis=1).astype(F32)).astype(BF16)
    w.drain()


def scatter(w, dev_at, sub, hid, wd, PB, SB, RB, FB, G1, G3, HB, JB):
    def blocks(rx, ry, target, core, extra):
        @pl.loop(0, 4, unroll=4)
        def _(rz):
            col = pl.multiple_of(dev_at(rx, ry, rz) * 512 + core * 256, 256)
            part = jnp.dot(hid[rx % 2], wd[:, pl.ds(col, 256)], preferred_element_type=F32)
            for h in (0, 1):
                one = part[:, h * 128:(h + 1) * 128]
                if extra is not None:
                    one = one + extra[rz, h].astype(F32)
                target[rz, h] = one.astype(BF16)

    def add(target, sources, p, count, where, half=None):
        _, h, (r0, r1), halves = PARTS[p]
        if half is not None:
            h, (r0, r1) = halves[half]
        hs = (0, 1) if isinstance(h, slice) else (h,)

        def one(i):
            t, ss = where(i)
            for hh in hs:
                total = target[tuple(t) + (hh, slice(r0, r1))].astype(F32)
                for source, s in zip(sources, ss):
                    total = total + source[tuple(s) + (hh, slice(r0, r1))].astype(F32)
                target[tuple(t) + (hh, slice(r0, r1))] = total.astype(BF16)

        if count == 1:
            one(0)
        else:
            pl.loop(0, count, unroll=count)(one)

    def cell(c, i):
        return {"0": (0, 0), "1": (i + 1, 0), "2": (0, i + 1), "3": (i + 1, 1), "4": (i + 1, 2), "5": (i + 1, 3)}[c]

    count = {"0": 1, "1": 3, "2": 3, "3": 3, "4": 3, "5": 3}

    def spot(p, a, b, c):
        dims = PARTS[p][0]
        r = [None] * 3
        r[dims[0]], r[dims[1]], r[dims[2]] = a, b, c
        return tuple(r)

    first, second, third, fourth = {}, {}, {}, {}
    order = "435120"
    units = [(2, 2), (2, 1), (2, 3), (2, 0), (3, 2), (1, 2), (0, 2), (3, 3), (1, 3), (3, 1), (1, 1), (0, 1), (0, 3), (3, 0), (1, 0), (0, 0)]
    swap, waiting = {}, []
    for c in order:
        for p in (1, 2, 0):
            for c3 in (2, 1, 3):
                need = set()
                for i in range(count[c]):
                    need.add(spot(p, *cell(c, i), c3)[:2])
                waiting.append((c3 != 2, p, c, c3, need))
    waiting.sort(key=lambda m: m[0])

    def far_core(u):
        rx, ry = units[u]
        if u >= 8:
            w.sent(swap[u - 8])
        blocks(rx, ry, SB.at[u % 8], 1 - sub, None)
        swap[u] = w.post(SB.at[u % 8], RB.at[rx, ry], None, 0)

    def near_core(u):
        swap[u].wait_recv()
        rx, ry = units[u]
        blocks(rx, ry, PB.at[rx, ry], sub, RB.at[rx, ry])
        done = set(units[:u + 1])
        for message in list(waiting):
            _, p, c, c3, need = message
            if not need <= done:
                continue
            waiting.remove(message)
            a, b = CHUNKS[c]
            d3 = PARTS[p][0][2]
            lead, f = lay(p, a, b), FLIP[c]
            if c3 == 2:
                first[p, c] = [
                    w.post(block(PB, p, a, b, 2, half=f), flat(FB, p, lead, f), d3, 1),
                    w.post(block(PB, p, a, b, 2, half=1 - f), flat(FB, p, lead, 1 - f), d3, 3),
                ]
            elif c3 == 1:
                second.setdefault((p, c), []).append(w.post(block(PB, p, a, b, 1, half=1 - f), flat(G1, p, lead, 1 - f), d3, 1))
            else:
                second.setdefault((p, c), []).append(w.post(block(PB, p, a, b, 3, half=f), flat(G3, p, lead, f), d3, 3))

    lag = 4
    for u in range(16 + lag):
        if u < 16:
            far_core(u)
        if u >= lag:
            near_core(u - lag)

    def pass_on(c):
        a, b = CHUNKS[c]
        for p in (1, 0, 2):
            d3 = PARTS[p][0][2]
            f = FLIP[c]
            for q, c3 in ((0, 1), (1, 3)):
                first[p, c][q].wait_recv()
                add(PB, (FB,), p, count[c], lambda i: (spot(p, *cell(c, i), c3), (lay(p, *cell(c, i)),)), half=q ^ f)
            second[p, c] += [
                w.post(block(PB, p, a, b, 1, half=f), flat(G1, p, lay(p, a, b), f), d3, 1),
                w.post(block(PB, p, a, b, 3, half=1 - f), flat(G3, p, lay(p, a, b), 1 - f), d3, 3),
            ]

    def collect(c):
        a, b = CHUNKS[c]
        for p in (1, 0, 2):
            d2 = PARTS[p][0][1]
            for copy in second[p, c]:
                copy.wait_recv()
            add(PB, (G1, G3), p, count[c], lambda i: (spot(p, *cell(c, i), 0), (lay(p, *cell(c, i)),) * 2))
            if c in "345":
                third[p, b] = w.post(block(PB, p, a, b, 0), flat(HB, p, (b - 1, a)), d2, b)
            if c == "2":
                third[p, 0] = [w.post(block(PB, p, 0, k, 0), flat(HB, p, (k - 1, 0)), d2, k) for k in (1, 3, 2)]

    for c in order:
        pass_on(c)
    for c in order:
        collect(c)
    for p in (1, 0, 2):
        d1 = PARTS[p][0][0]
        for k in (2, 1, 3):
            third[p, k].wait_recv()
        add(PB, (HB,) * 3, p, 3, lambda i: (spot(p, i + 1, 0, 0), tuple((k, i + 1) for k in range(3))))
        fourth[p] = [w.post(block(PB, p, k, 0, 0), flat(JB, p, (k - 1,)), d1, k) for k in (1, 3, 2)]
    for p in (1, 0, 2):
        for copy in third[p, 0]:
            copy.wait_recv()
        add(PB, (HB,) * 3, p, 1, lambda i: (spot(p, 0, 0, 0), tuple((k, 0) for k in range(3))))
    for p in (1, 0, 2):
        for copy in fourth[p]:
            copy.wait_recv()
        add(PB, (JB,) * 3, p, 1, lambda i: (spot(p, 0, 0, 0), tuple((k,) for k in range(3))))


def ffn(q, nk, nv, kc, vc, lengths, res, wo, gain, wg, wu, wd):
    hbm = pl.BlockSpec(memory_space=pl.ANY)
    vmem = pl.BlockSpec(memory_space=pltpu.VMEM)
    smem = pl.BlockSpec(memory_space=pltpu.SMEM)
    grid = (4, 4, 4)
    tail = (2, ROWS, 128)
    return pl.pallas_call(
        ffn_kernel,
        out_shape=jax.ShapeDtypeStruct((ROWS, 256), BF16),
        in_specs=[vmem, vmem, vmem, hbm, hbm, smem, vmem, hbm, vmem, hbm, hbm, hbm],
        out_specs=vmem,
        scratch_shapes=[
            pltpu.VMEM((5, CACHE, 256), BF16),
            pltpu.VMEM((5, CACHE, 256), BF16),
            pltpu.VMEM((4096, 512), BF16),
            pltpu.VMEM((ROWS, 128), F32),
            pltpu.VMEM((2, 4, 4, ROWS, 128), BF16),
            pltpu.VMEM((32 * ROWS, 128), F32),
            pltpu.VMEM((2, ROWS, 256), BF16),
            pltpu.VMEM((ROWS, 256), BF16),
            pltpu.VMEM((2, ROWS, 256), F32),
            pltpu.VMEM(grid + (2,) + tail, BF16),
            pltpu.VMEM(grid + tail, BF16),
            pltpu.VMEM((8, 4) + tail, BF16),
            pltpu.VMEM(grid + tail, BF16),
            pltpu.VMEM((4, 4) + tail, BF16),
            pltpu.VMEM((4, 4) + tail, BF16),
            pltpu.VMEM((4, 4) + tail, BF16),
            pltpu.VMEM((3, 4) + tail, BF16),
            pltpu.VMEM((3,) + tail, BF16),
            pltpu.VMEM((5, 8, 256), F32),
            pltpu.VMEM((13, 8, 256), F32),
            pltpu.VMEM((HID, D), BF16),
            pltpu.VMEM((HID, D), BF16),
            pltpu.VMEM((HID, D), BF16),
            pltpu.VMEM((2, 2 * ROWS, HID), F32),
            pltpu.VMEM((2, ROWS, HID), BF16),
            pltpu.SemaphoreType.DMA((6,)),
            pltpu.SemaphoreType.DMA((360,)),
            pltpu.SemaphoreType.DMA((360,)),
        ],
        compiler_params=pltpu.CompilerParams(
            collective_id=1, has_side_effects=True, vmem_limit_bytes=62 * 2**20
        ),
        name="ffn",
    )(q, nk, nv, kc, vc, lengths, res, wo, gain, wg, wu, wd)


def shards(
    queries,
    new_keys,
    new_values,
    key_cache,
    value_cache,
    lengths,
    residual,
    o_weight,
    norm_gain,
    w_gate,
    w_up,
    w_down,
):
    return ffn(
        queries, new_keys, new_values, key_cache, value_cache, lengths, residual,
        o_weight, norm_gain, w_gate, w_up, w_down,
    )


def solution(mesh):
    placed = (
        P(("grp", "dev"), "sub"),
        P(("grp", "dev"), "sub"),
        P(("grp", "dev"), "sub"),
        P(("grp", "dev"), None, "sub"),
        P(("grp", "dev"), None, "sub"),
        P(("grp", "dev")),
        P("grp", ("dev", "sub")),
        P("sub", "dev"),
        P(("dev", "sub")),
        P(("grp", "dev", "sub"), None),
        P(("grp", "dev", "sub"), None),
        P(("grp", "dev", "sub"), None),
    )
    return jax.shard_map(
        shards, mesh=mesh, in_specs=placed, out_specs=P("grp", ("dev", "sub")), check_vma=False
    )
```

```python
import functools

import jax
import jax.numpy as jnp
from jax import lax
from jax.experimental import pallas as pl
from jax.experimental.pallas import tpu as pltpu
from jax.sharding import PartitionSpec as P

D = 16384
HEAD_DIM = 128
MESH = pl.DeviceIdType.MESH
F32, BF16 = jnp.float32, jnp.bfloat16
ROWS, HID, CACHE = 160, 208, 384
CHUNKS = {
    "0": (0, 0), "1": (slice(1, 4), 0), "2": (0, slice(1, 4)),
    "3": (slice(1, 4), 1), "4": (slice(1, 4), 2), "5": (slice(1, 4), 3),
}
FLIP = {"0": 0, "1": 1, "2": 0, "3": 0, "4": 1, "5": 0}
PARTS = (
    ((0, 1, 2), 0, (0, 112), ((0, (0, 64)), (0, (64, 112)))),
    ((1, 2, 0), 1, (0, 112), ((1, (0, 64)), (1, (64, 112)))),
    ((2, 0, 1), slice(0, 2), (112, 160), ((0, (112, 160)), (1, (112, 160)))),
)


def place():
    grp, dev, sub = lax.axis_index("grp"), lax.axis_index("dev"), lax.axis_index("sub")
    return [(dev // 16) * 2 + grp, dev % 4, (dev // 4) % 4], sub


def device(at, sub):
    x, y, z = at
    return (lax.rem(x, 2), (x // 2) * 16 + z * 4 + y, sub)


def shifted(at, dim, by):
    at = list(at)
    at[dim] = lax.rem(at[dim] + by, 4)
    return at


class Wires:
    def __init__(self, at, sub, send, recv):
        self.at, self.sub, self.send, self.recv, self.n = at, sub, send, recv, 0
        self.started = []

    def post(self, src, dst, dim, by, over=0):
        if dim is None:
            to = device(self.at, 1 - self.sub)
        else:
            to = device(shifted(shifted(self.at, dim, by), 0, over), self.sub)
        copy = pltpu.make_async_remote_copy(
            src_ref=src, dst_ref=dst, send_sem=self.send.at[self.n], recv_sem=self.recv.at[self.n],
            device_id=to, device_id_type=MESH,
        )
        copy.start()
        self.n += 1
        self.started.append(copy)
        return copy

    def sent(self, copy):
        copy.wait_send()
        self.started = [c for c in self.started if c is not copy]

    def drain(self):
        for copy in self.started:
            copy.wait_send()
        self.started = []


def block(buf, part, a, b, c, tail=(), half=None):
    dims, h, rows, halves = PARTS[part]
    if half is not None:
        h, rows = halves[half]
    idx = [None] * 3
    idx[dims[0]], idx[dims[1]], idx[dims[2]] = a, b, c
    return buf.at[tuple(idx) + tuple(tail) + (h, slice(*rows), slice(None))]


def lay(part, a, b):
    return (b, a) if part == 2 else (a, b)


def flat(buf, part, lead, half=None):
    _, h, rows, halves = PARTS[part]
    if half is not None:
        h, rows = halves[half]
    return buf.at[tuple(lead) + (h, slice(*rows), slice(None))]


def gather(w, XB, sq, ready):
    m1, m2a, m2b, m3, fwd = {}, {}, {}, {}, {}
    own = lambda p: block(XB, p, 0, 0, 0, (0,))
    xb = lambda p, a, b, c, half=None, s=0: block(XB, p, a, b, c, (s,), half)
    d2d = []

    def plane(p, c, up=True):
        a, b = CHUNKS[c]
        d3 = PARTS[p][0][2]
        m3[p, c] = [
            w.post(xb(p, a, b, 0), xb(p, a, b, 3), d3, 1),
            w.post(xb(p, a, b, 0), xb(p, a, b, 1), d3, 3),
        ]

    def onward(p, c):
        a, b = CHUNKS[c]
        d3 = PARTS[p][0][2]
        f = FLIP[c]
        for copy in m3[p, c]:
            copy.wait_recv()
        fwd[p, c] = [
            w.post(xb(p, a, b, 3, f), xb(p, a, b, 2, f), d3, 1),
            w.post(xb(p, a, b, 1, 1 - f), xb(p, a, b, 2, 1 - f), d3, 3),
        ]

    def landed(copies):
        for copy in copies:
            copy.wait_recv()

    def across(p, a, b, c):
        d2d.append(w.post(xb(p, a, b, c), xb(p, a, b, c, s=1), None, 0))

    for p in range(3):
        d1 = PARTS[p][0][0]
        m1[p] = [w.post(own(p), xb(p, 4 - k, 0, 0), d1, k) for k in (1, 3, 2)]
    for p in range(3):
        d2 = PARTS[p][0][1]
        m2a[p] = [w.post(own(p), xb(p, 0, 4 - k, 0), d2, k) for k in (1, 3, 2)]
    for p in range(3):
        plane(p, "0")
    sq(0)
    for p in range(3):
        d2 = PARTS[p][0][1]
        for copy in m1[p]:
            copy.wait_recv()
        m2b[p] = [w.post(xb(p, slice(1, 4), 0, 0), xb(p, slice(1, 4), 4 - k, 0), d2, k) for k in (1, 3, 2)]
    for p in range(3):
        plane(p, "1")
    for p in range(3):
        for copy in m2a[p]:
            copy.wait_recv()
        plane(p, "2")
        across(p, slice(0, 4), 0, 0)
    sq(1)
    for p in range(3):
        onward(p, "0")
    for i, c in enumerate("53"):
        for p in range(3):
            m2b[p][i].wait_recv()
            plane(p, c)
    sq(2)
    for p in range(3):
        m2b[p][2].wait_recv()
        plane(p, "4")
        across(p, slice(0, 4), slice(1, 4), 0)
    for c in "12":
        for p in range(3):
            onward(p, c)
    sq(3)
    for p in range(3):
        onward(p, "5")
    for p in range(3):
        for c in "012":
            for copy in fwd[p, c]:
                copy.wait_recv()
        across(p, slice(0, 4), 0, slice(1, 4))
        across(p, 0, slice(1, 4), slice(1, 4))
    early = list(d2d)
    d2d.clear()
    for p in range(3):
        onward(p, "3")
    for p in range(3):
        onward(p, "4")
        across(p, slice(1, 4), slice(1, 4), 1)
        across(p, slice(1, 4), slice(1, 4), 3)
    sq(4)
    landed(early)
    for step in range(4):
        ready(step)
    landed(d2d)
    ready(4)
    late = {}
    for r2, c in ((3, "5"), (1, "3"), (2, "4")):
        if c == "4":
            landed(late["5"])
            ready(5)
        n = len(d2d)
        for p in range(3):
            for copy in fwd[p, c]:
                copy.wait_recv()
            across(p, slice(1, 4), r2, 2)
        late[c] = d2d[n:]
    landed(late["3"])
    ready(6)
    ready(7)
    landed(late["4"])
    ready(8)
    ready(9)


def attention(q_ref, nk_ref, nv_ref, kc, vc, len_ref, qs, CB):
    for h in range(32):
        qs[pl.ds(h, 5, stride=32), :] = q_ref[:, h * 128:(h + 1) * 128].astype(F32)
    span = lax.broadcasted_iota(jnp.int32, (16, CACHE), 1)
    scale = 1.0 / HEAD_DIM**0.5
    for b in range(5):
        for g in range(2):
            cols = slice(g * 128, (g + 1) * 128)
            q = qs[b * 32 + g * 16:b * 32 + (g + 1) * 16]
            scores = lax.dot_general(
                q.astype(BF16), kc[b, :, cols], (((1,), (1,)), ((), ())), preferred_element_type=F32
            ) * scale
            own = jnp.sum(q * nk_ref[b:b + 1, cols].astype(F32), axis=1, keepdims=True) * scale
            valid = span < len_ref[b]
            masked = jnp.where(valid, scores, -1e30)
            top = jnp.maximum(jnp.max(masked, axis=1, keepdims=True), own)
            weights = jnp.where(valid, jnp.exp(masked - top), 0.0)
            own = jnp.exp(own - top)
            total = jnp.sum(weights, axis=1, keepdims=True) + own
            probs = (weights / total).astype(BF16)
            own = (own / total).astype(BF16).astype(F32)
            context = jnp.dot(probs, vc[b, :, cols], preferred_element_type=F32)
            context = context + own * nv_ref[b:b + 1, cols].astype(F32)
            CB[0, 0, 0, b * 32 + g * 16:b * 32 + (g + 1) * 16] = context.astype(BF16)


def project(w, at, sub, CB, LH, wo, wo_load, half_out, half_in):
    x0, y0, z0 = at

    def part(q, rx, ry, rz):
        return CB.at[rx, ry, rz, q * 80:(q + 1) * 80]

    def cut(q, rx, a, b):
        return part(q, rx, *((b, a) if q == 0 else (a, b)))

    dims = ((2, 1), (1, 2))
    turns = (1, 3, 2)
    both = slice(0, 2)

    def settle(rx, ry, rz):
        dev = (lax.rem(x0 + 2 * rx, 4) // 2) * 16 + lax.rem(z0 + rz, 4) * 4 + lax.rem(y0 + ry, 4)
        for b in range(5):
            LH[pl.ds(dev * 5 + b, 32, stride=ROWS), :] = CB[rx, ry, rz, b * 32:(b + 1) * 32].astype(F32)

    planes = [[], []]

    def plane(q, rx, r):
        planes[q] += [w.post(cut(q, rx, r, 0), cut(q, rx, r, 4 - k), dims[q][1], k) for k in turns]

    hop = [w.post(part(q, 0, 0, 0), part(q, 1, 0, 0), 0, 2) for q in range(2)]
    near = [[w.post(cut(q, 0, 0, 0), cut(q, 0, 4 - k, 0), dims[q][0], k) for k in turns] for q in range(2)]
    far = [[w.post(cut(q, 0, 0, 0), cut(q, 1, 4 - k, 0), dims[q][0], k, over=2) for k in turns] for q in range(2)]
    for q in range(2):
        plane(q, 0, 0)
    settle(0, 0, 0)
    for i in range(3):
        for q in range(2):
            near[q][i].wait_recv()
            plane(q, 0, 4 - turns[i])
    for q in range(2):
        hop[q].wait_recv()
        plane(q, 1, 0)
    settle(1, 0, 0)
    for i in range(3):
        for q in range(2):
            far[q][i].wait_recv()
            plane(q, 1, 4 - turns[i])
    for q in range(2):
        for copy in planes[q]:
            copy.wait_recv()

    @pl.loop(0, 30)
    def _(i):
        i = i + 1 + i // 15
        settle(i // 16, (i // 4) % 4, i % 4)

    wo_load.wait()

    lhs = jnp.concatenate([LH[h * ROWS:(h + 1) * ROWS, :].astype(BF16) for h in range(32)], axis=1)

    def half(core):
        return jnp.dot(lhs, wo[:, pl.ds(pl.multiple_of(core * 256, 256), 256)], preferred_element_type=F32)

    half_out[...] = half(1 - sub).astype(BF16)
    swap = w.post(half_out, half_in, None, 0)
    mine = half(sub)
    swap.wait_recv()
    return mine + half_in[...].astype(F32)


def ffn_kernel(q_ref, nk_ref, nv_ref, kc_hbm, vc_hbm, len_ref, res_ref, wo_hbm, gain_ref, wg_hbm, wu_hbm, wd_hbm, out_ref,
               kc, vc, wo, qs, CB, LH, half_out, half_in, mid_ref,
               XB, PB, SB, RB, FB, G1, G3, HB, JB, sqs, sqr, wg, wu, wd, acc, hid, wsem, send, recv):
    at, sub = place()
    x0, y0, z0 = at
    grp = lax.rem(x0, 2)
    w = Wires(at, sub, send, recv)
    pairs = ((wg_hbm, wg), (wu_hbm, wu), (wd_hbm, wd), (kc_hbm, kc), (vc_hbm, vc), (wo_hbm, wo))
    loads = [pltpu.make_async_copy(a, b, wsem.at[i]) for i, (a, b) in enumerate(pairs)]
    loads = [loads[i] for i in (3, 4, 5, 0, 1, 2)]
    for load in loads:
        load.start()
    barrier = pltpu.get_barrier_semaphore()
    for dim in range(3):
        for by in (1, 2, 3):
            pl.semaphore_signal(barrier, inc=1, device_id=device(shifted(at, dim, by), sub), device_id_type=MESH)
    for dim in (1, 2):
        for by in (1, 2, 3):
            to = device(shifted(shifted(at, dim, by), 0, 2), sub)
            pl.semaphore_signal(barrier, inc=1, device_id=to, device_id_type=MESH)
    pl.semaphore_signal(barrier, inc=1, device_id=device(at, 1 - sub), device_id_type=MESH)

    loads[0].wait()
    loads[1].wait()
    attention(q_ref, nk_ref, nv_ref, kc, vc, len_ref, qs, CB)
    pl.semaphore_wait(barrier, 16)
    mid = project(w, at, sub, CB, LH, wo, loads[2], half_out, half_in) + res_ref[...].astype(F32)
    mid_ref[...] = mid
    loads = loads[3:]

    rows = (mid * gain_ref[...].astype(F32)[None, :]).astype(BF16)
    XB[0, 0, 0, 0, 0] = rows[:, :128]
    XB[0, 0, 0, 0, 1] = rows[:, 128:]
    eye = lax.broadcasted_iota(jnp.int32, (ROWS, 256), 0) == lax.broadcasted_iota(jnp.int32, (ROWS, 256), 1)
    column = jnp.sum(mid * mid, axis=1, keepdims=True)
    sqs[0] = jnp.broadcast_to(jnp.sum(jnp.where(eye, column, 0.0), axis=0, keepdims=True), (8, 256))

    sq_copies = {}

    def sq(step):
        if step > 0:
            total = sqs[step - 1]
            for i, copy in enumerate(sq_copies[step - 1]):
                copy.wait_recv()
                total = total + sqr[(step - 1) * 3 + i]
            sqs[step] = total
        if step == 0:
            sq_copies[0] = [w.post(sqs.at[0], sqr.at[0], None, 0)]
        elif step == 1:
            sq_copies[1] = [w.post(sqs.at[1], sqr.at[3 + i], 1, k) for i, k in enumerate((1, 3, 2))]
        elif step == 2:
            sq_copies[2] = [w.post(sqs.at[2], sqr.at[6 + i], 2, k) for i, k in enumerate((1, 3, 2))]
        elif step == 3:
            sq_copies[3] = [w.post(sqs.at[3], sqr.at[9], 0, 2)]
        else:
            sq_copies[4] = [w.post(sqs.at[4], sqr.at[12], 0, 1)]

    def dev_at(rx, ry, rz):
        return (lax.rem(x0 + rx, 4) // 2) * 16 + lax.rem(z0 + rz, 4) * 4 + lax.rem(y0 + ry, 4)

    corner = [(r, 0, rz) for r in (0, 2) for rz in range(4)] + [(r, ry, 0) for r in (0, 2) for ry in (1, 2, 3)]
    odd = [(0, ry, rz) for ry in (1, 3) for rz in (1, 3)]
    batches = {0: corner[0:4], 1: corner[4:8], 2: corner[8:11], 3: corner[11:14], 4: odd,
               5: [(2, 1, 3), (2, 3, 3), (0, 3, 2)], 6: [(2, 1, 1), (2, 3, 1), (0, 1, 2)], 7: [(0, 2, 1), (0, 2, 3)],
               8: [(2, 2, 1), (2, 2, 3), (2, 2, 2)], 9: [(2, 1, 2), (2, 3, 2), (0, 2, 2)]}

    def ready(step):
        if step == 0:
            loads[0].wait()
            loads[1].wait()
        pairs = [(rx, lax.rem(rx + 5 - 2 * grp, 4), ry, rz) for rx, ry, rz in batches[step]]
        ks = [pl.multiple_of(dev_at(rx, ry, rz) * 512, 512) for rx, _, ry, rz in pairs]
        lhs = jnp.concatenate(
            [
                jnp.concatenate(
                    [XB[pair[q], pair[2], pair[3], s, h] for pair in pairs for s in (sub, 1 - sub) for h in (0, 1)], axis=1
                )
                for q in (0, 1)
            ],
            axis=0,
        )
        for j, weight in enumerate((wg, wu)):
            rhs = jnp.concatenate([weight[:, pl.ds(k, 512)] for k in ks], axis=1)
            part = lax.dot_general(lhs, rhs, (((1,), (1,)), ((), ())), preferred_element_type=F32)
            acc[j] = part if step == 0 else acc[j] + part

    gather(w, XB, sq, ready)

    sq_copies[4][0].wait_recv()
    for i, sums in enumerate((sqs[4], sqr[12])):
        inv_row = lax.rsqrt(sums[0:1] / D + 1e-05)
        inv = jnp.sum(jnp.where(eye, inv_row, 0.0), axis=1, keepdims=True)
        gate = acc[0, i * ROWS:(i + 1) * ROWS] * inv
        up = acc[1, i * ROWS:(i + 1) * ROWS] * inv
        hid[i] = (gate / (1.0 + jnp.exp(-gate)) * up).astype(BF16)
    loads[2].wait()
    scatter(w, dev_at, sub, hid, wd, PB, SB, RB, FB, G1, G3, HB, JB)
    out_ref[...] = (mid_ref[...] + jnp.concatenate([PB[0, 0, 0, 0], PB[0, 0, 0, 1]], axis=1).astype(F32)).astype(BF16)
    w.drain()


def scatter(w, dev_at, sub, hid, wd, PB, SB, RB, FB, G1, G3, HB, JB):
    def blocks(rx, ry, target, core, extra):
        @pl.loop(0, 4, unroll=4)
        def _(rz):
            col = pl.multiple_of(dev_at(rx, ry, rz) * 512 + core * 256, 256)
            part = jnp.dot(hid[rx % 2], wd[:, pl.ds(col, 256)], preferred_element_type=F32)
            for h in (0, 1):
                one = part[:, h * 128:(h + 1) * 128]
                if extra is not None:
                    one = one + extra[rz, h].astype(F32)
                target[rz, h] = one.astype(BF16)

    def add(target, sources, p, count, where, half=None):
        _, h, (r0, r1), halves = PARTS[p]
        if half is not None:
            h, (r0, r1) = halves[half]
        hs = (0, 1) if isinstance(h, slice) else (h,)

        def one(i):
            t, ss = where(i)
            for hh in hs:
                total = target[tuple(t) + (hh, slice(r0, r1))].astype(F32)
                for source, s in zip(sources, ss):
                    total = total + source[tuple(s) + (hh, slice(r0, r1))].astype(F32)
                target[tuple(t) + (hh, slice(r0, r1))] = total.astype(BF16)

        if count == 1:
            one(0)
        else:
            pl.loop(0, count, unroll=count)(one)

    def cell(c, i):
        return {"0": (0, 0), "1": (i + 1, 0), "2": (0, i + 1), "3": (i + 1, 1), "4": (i + 1, 2), "5": (i + 1, 3)}[c]

    count = {"0": 1, "1": 3, "2": 3, "3": 3, "4": 3, "5": 3}

    def spot(p, a, b, c):
        dims = PARTS[p][0]
        r = [None] * 3
        r[dims[0]], r[dims[1]], r[dims[2]] = a, b, c
        return tuple(r)

    first, second, third, fourth = {}, {}, {}, {}
    order = "435120"
    units = [(2, 2), (2, 1), (2, 3), (2, 0), (3, 2), (1, 2), (0, 2), (3, 3), (1, 3), (3, 1), (1, 1), (0, 1), (0, 3), (3, 0), (1, 0), (0, 0)]
    swap, waiting = {}, []
    for c in order:
        for p in (1, 2, 0):
            for c3 in (2, 1, 3):
                need = set()
                for i in range(count[c]):
                    need.add(spot(p, *cell(c, i), c3)[:2])
                waiting.append((c3 != 2, p, c, c3, need))
    waiting.sort(key=lambda m: m[0])

    def far_core(u):
        rx, ry = units[u]
        if u >= 8:
            w.sent(swap[u - 8])
        blocks(rx, ry, SB.at[u % 8], 1 - sub, None)
        swap[u] = w.post(SB.at[u % 8], RB.at[rx, ry], None, 0)

    def near_core(u):
        swap[u].wait_recv()
        rx, ry = units[u]
        blocks(rx, ry, PB.at[rx, ry], sub, RB.at[rx, ry])
        done = set(units[:u + 1])
        for message in list(waiting):
            _, p, c, c3, need = message
            if not need <= done:
                continue
            waiting.remove(message)
            a, b = CHUNKS[c]
            d3 = PARTS[p][0][2]
            lead, f = lay(p, a, b), FLIP[c]
            if c3 == 2:
                first[p, c] = [
                    w.post(block(PB, p, a, b, 2, half=f), flat(FB, p, lead, f), d3, 1),
                    w.post(block(PB, p, a, b, 2, half=1 - f), flat(FB, p, lead, 1 - f), d3, 3),
                ]
            elif c3 == 1:
                second.setdefault((p, c), []).append(w.post(block(PB, p, a, b, 1, half=1 - f), flat(G1, p, lead, 1 - f), d3, 1))
            else:
                second.setdefault((p, c), []).append(w.post(block(PB, p, a, b, 3, half=f), flat(G3, p, lead, f), d3, 3))

    lag = 4
    for u in range(16 + lag):
        if u < 16:
            far_core(u)
        if u >= lag:
            near_core(u - lag)

    def pass_on(c):
        a, b = CHUNKS[c]
        for p in (1, 0, 2):
            d3 = PARTS[p][0][2]
            f = FLIP[c]
            for q, c3 in ((0, 1), (1, 3)):
                first[p, c][q].wait_recv()
                add(PB, (FB,), p, count[c], lambda i: (spot(p, *cell(c, i), c3), (lay(p, *cell(c, i)),)), half=q ^ f)
            second[p, c] += [
                w.post(block(PB, p, a, b, 1, half=f), flat(G1, p, lay(p, a, b), f), d3, 1),
                w.post(block(PB, p, a, b, 3, half=1 - f), flat(G3, p, lay(p, a, b), 1 - f), d3, 3),
            ]

    def collect(c):
        a, b = CHUNKS[c]
        for p in (1, 0, 2):
            d2 = PARTS[p][0][1]
            for copy in second[p, c]:
                copy.wait_recv()
            add(PB, (G1, G3), p, count[c], lambda i: (spot(p, *cell(c, i), 0), (lay(p, *cell(c, i)),) * 2))
            if c in "345":
                third[p, b] = w.post(block(PB, p, a, b, 0), flat(HB, p, (b - 1, a)), d2, b)
            if c == "2":
                third[p, 0] = [w.post(block(PB, p, 0, k, 0), flat(HB, p, (k - 1, 0)), d2, k) for k in (1, 3, 2)]

    for kind, c in zip("PPPPPCPCCCCC", "435124035120"):
        (pass_on if kind == "P" else collect)(c)
    for p in (1, 0, 2):
        d1 = PARTS[p][0][0]
        for k in (2, 1, 3):
            third[p, k].wait_recv()
        add(PB, (HB,) * 3, p, 3, lambda i: (spot(p, i + 1, 0, 0), tuple((k, i + 1) for k in range(3))))
        fourth[p] = [w.post(block(PB, p, k, 0, 0), flat(JB, p, (k - 1,)), d1, k) for k in (1, 3, 2)]
    for p in (1, 0, 2):
        for copy in third[p, 0]:
            copy.wait_recv()
        add(PB, (HB,) * 3, p, 1, lambda i: (spot(p, 0, 0, 0), tuple((k, 0) for k in range(3))))
    for p in (1, 0, 2):
        for copy in fourth[p]:
            copy.wait_recv()
        add(PB, (JB,) * 3, p, 1, lambda i: (spot(p, 0, 0, 0), tuple((k,) for k in range(3))))


def ffn(q, nk, nv, kc, vc, lengths, res, wo, gain, wg, wu, wd):
    hbm = pl.BlockSpec(memory_space=pl.ANY)
    vmem = pl.BlockSpec(memory_space=pltpu.VMEM)
    smem = pl.BlockSpec(memory_space=pltpu.SMEM)
    grid = (4, 4, 4)
    tail = (2, ROWS, 128)
    return pl.pallas_call(
        ffn_kernel,
        out_shape=jax.ShapeDtypeStruct((ROWS, 256), BF16),
        in_specs=[vmem, vmem, vmem, hbm, hbm, smem, vmem, hbm, vmem, hbm, hbm, hbm],
        out_specs=vmem,
        scratch_shapes=[
            pltpu.VMEM((5, CACHE, 256), BF16),
            pltpu.VMEM((5, CACHE, 256), BF16),
            pltpu.VMEM((4096, 512), BF16),
            pltpu.VMEM((ROWS, 128), F32),
            pltpu.VMEM((2, 4, 4, ROWS, 128), BF16),
            pltpu.VMEM((32 * ROWS, 128), F32),
            pltpu.VMEM((ROWS, 256), BF16),
            pltpu.VMEM((ROWS, 256), BF16),
            pltpu.VMEM((ROWS, 256), F32),
            pltpu.VMEM(grid + (2,) + tail, BF16),
            pltpu.VMEM(grid + tail, BF16),
            pltpu.VMEM((8, 4) + tail, BF16),
            pltpu.VMEM(grid + tail, BF16),
            pltpu.VMEM((4, 4) + tail, BF16),
            pltpu.VMEM((4, 4) + tail, BF16),
            pltpu.VMEM((4, 4) + tail, BF16),
            pltpu.VMEM((3, 4) + tail, BF16),
            pltpu.VMEM((3,) + tail, BF16),
            pltpu.VMEM((5, 8, 256), F32),
            pltpu.VMEM((13, 8, 256), F32),
            pltpu.VMEM((HID, D), BF16),
            pltpu.VMEM((HID, D), BF16),
            pltpu.VMEM((HID, D), BF16),
            pltpu.VMEM((2, 2 * ROWS, HID), F32),
            pltpu.VMEM((2, ROWS, HID), BF16),
            pltpu.SemaphoreType.DMA((6,)),
            pltpu.SemaphoreType.DMA((360,)),
            pltpu.SemaphoreType.DMA((360,)),
        ],
        compiler_params=pltpu.CompilerParams(
            collective_id=1, has_side_effects=True, vmem_limit_bytes=62 * 2**20
        ),
        name="ffn",
    )(q, nk, nv, kc, vc, lengths, res, wo, gain, wg, wu, wd)


def shards(
    queries,
    new_keys,
    new_values,
    key_cache,
    value_cache,
    lengths,
    residual,
    o_weight,
    norm_gain,
    w_gate,
    w_up,
    w_down,
):
    return ffn(
        queries, new_keys, new_values, key_cache, value_cache, lengths, residual,
        o_weight, norm_gain, w_gate, w_up, w_down,
    )


def solution(mesh):
    placed = (
        P(("grp", "dev"), "sub"),
        P(("grp", "dev"), "sub"),
        P(("grp", "dev"), "sub"),
        P(("grp", "dev"), None, "sub"),
        P(("grp", "dev"), None, "sub"),
        P(("grp", "dev")),
        P("grp", ("dev", "sub")),
        P("sub", "dev"),
        P(("dev", "sub")),
        P(("grp", "dev", "sub"), None),
        P(("grp", "dev", "sub"), None),
        P(("grp", "dev", "sub"), None),
    )
    return jax.shard_map(
        shards, mesh=mesh, in_specs=placed, out_specs=P("grp", ("dev", "sub")), check_vma=False
    )
```
